256 devices in a mesh: replica: 8 (over y, core), fsdp: 32 (over z, x).
Axes of the slice: x: 4, y: 4, z: 8, core: 2. Of those that a mesh axis runs over, the one named last changes fastest.
Arguments:
- grads: bfloat16 [8, 4, 1024, 8192], P('replica', None, 'fsdp'), may hold values from -32 to 32
- left_root: bfloat16 [64, 1024, 1024], P('fsdp'), may hold values from -1 to 2.5
- right_root: bfloat16 [64, 1024, 1024], P('fsdp'), may hold values from -1 to 2.5
- block_slot: int32 [32], replicated, may hold values from 0 to 63, as said below
Outputs:
- updates: bfloat16 [4, 1024, 8192], P(None, 'fsdp')
The draws below stay inside these ranges and needn't reach their ends.
Inputs may be any that keep to these rules, and one draw needn't show every extreme that they name: block_slot gives the 32 blocks distinct slots; slot q belongs to owner q // 2 of fsdp; some owners hold 2 blocks and as many hold none.
All inputs are finite; a program needn't handle non-finite values.
Results may differ from the reference program's by a relative error of at most 0.02.
Values may be sent and summed in bfloat16 or wider, within the bound.
No kernel may reach another device: no remote copies, remote signals or barrier semaphores. Data moves between devices by JAX's collectives and lax.ppermute only.
A program may use at most 128 MiB of HBM per device.

```python
import math
import jax
import jax.numpy as jnp
from jax import lax

D = 8192
KVW = 1024
B = 1024
SLOTS = 2
REPS = 8
MATS = 4
NCB = 8
NB = 32
OWNER_SLOTS = 64
N_FSDP = 32


def scale_profile(key, scale_shape, top_value):
    return jnp.exp(jax.random.uniform(key, scale_shape, jnp.float32, 0.0, math.log(top_value)))


def draw_grads(key, part):
    key = jax.random.fold_in(key, 11)
    key_base, key_rows, key_cols = jax.random.split(key, 3)
    grad_shape = (REPS, MATS, KVW, D)
    column_trend = 3.0 ** ((jnp.arange(D) % B).astype(jnp.float32) / B)
    column_scale = scale_profile(key_cols, (MATS, 1, D), 10.0) * column_trend
    fresh_noise = jnp.clip(jax.random.normal(key_base, grad_shape, jnp.float32), -4.0, 4.0)
    values = fresh_noise * scale_profile(key_rows, (MATS, KVW, 1), 10.0) * column_scale / 40.0
    return values.astype(jnp.bfloat16)


def factor_like(diag_key, noise_values, order_size):
    diagonal = scale_profile(diag_key, noise_values.shape[:2], 4.0) * 0.5
    symmetric = (noise_values + jnp.swapaxes(noise_values, 1, 2)) * (0.5 / math.sqrt(2.0 * order_size))
    identity = jnp.eye(order_size, dtype=jnp.float32)
    return (symmetric + diagonal[:, :, None] * identity[None, :, :]).astype(jnp.bfloat16)


def draw_left_root(key, part):
    key = jax.random.fold_in(key, 23)
    key_diag, key_noise = jax.random.split(key)
    factor_shape = (OWNER_SLOTS, KVW, KVW)
    noise_values = jnp.clip(jax.random.normal(key_noise, factor_shape, jnp.float32), -4.0, 4.0)
    return factor_like(key_diag, noise_values, KVW)


def draw_right_root(key, part):
    key = jax.random.fold_in(key, 29)
    key_diag, key_noise = jax.random.split(key)
    factor_shape = (OWNER_SLOTS, B, B)
    noise_values = jnp.clip(jax.random.normal(key_noise, factor_shape, jnp.float32), -4.0, 4.0)
    return factor_like(key_diag, noise_values, B)


def draw_block_slot(key, part):
    key = jax.random.fold_in(key, 37)
    key_full, key_order, key_shuffle = jax.random.split(key, 3)
    full_owners = jax.random.randint(key_full, (), 1, N_FSDP // 2 + 1)
    middle_owners = jax.random.permutation(key_order, N_FSDP - 2).astype(jnp.int32) + 1
    owner_order = jnp.concatenate([jnp.array([N_FSDP - 1], jnp.int32), jnp.array([0], jnp.int32), middle_owners])
    owner_rank = jnp.arange(N_FSDP, dtype=jnp.int32)[:, None]
    slot_pos = jnp.arange(SLOTS, dtype=jnp.int32)[None, :]
    in_use = (owner_rank < full_owners) | (owner_rank < N_FSDP - full_owners) & (slot_pos == 0)
    slot_value = owner_order[:, None] * SLOTS + slot_pos
    sort_key = jnp.where(in_use, 0, 1).reshape(-1) * (N_FSDP * SLOTS) + jnp.arange(N_FSDP * SLOTS, dtype=jnp.int32)
    picked = jnp.argsort(sort_key, stable=True)[:NB]
    chosen = slot_value.reshape(-1)[picked]
    return jax.random.permutation(key_shuffle, chosen).astype(jnp.int32)


def setup_inputs(seed: int = 0) -> dict:
    keys = jax.random.split(jax.random.key(seed), 5)
    return {
        "grads": draw_grads(jax.random.fold_in(keys[4], 71), 0),
        "left_root": draw_left_root(jax.random.fold_in(keys[4], 71), 0),
        "right_root": draw_right_root(jax.random.fold_in(keys[4], 71), 0),
        "block_slot": draw_block_slot(jax.random.fold_in(keys[4], 71), 0),
    }


EPSILON = 1e-06

def reference(grads, left_root, right_root, block_slot):
    summed_grad = lax.optimization_barrier(jnp.sum(grads.astype(jnp.float32), axis=0)).astype(jnp.bfloat16)
    blocks = summed_grad.reshape(MATS, KVW, NCB, B).transpose(0, 2, 1, 3).reshape(NB, KVW, B)

    def precondition_block(operands):
        block_grad, slot_index = operands
        left_factor = lax.dynamic_index_in_dim(left_root, slot_index, 0, keepdims=False)
        right_factor = lax.dynamic_index_in_dim(right_root, slot_index, 0, keepdims=False)
        right_half = jnp.dot(block_grad, right_factor, preferred_element_type=jnp.float32).astype(jnp.bfloat16)
        preconditioned = jnp.dot(left_factor, right_half, preferred_element_type=jnp.float32)
        grad_square = jnp.mean(jnp.square(block_grad.astype(jnp.float32)))
        prec_square = jnp.mean(jnp.square(preconditioned))
        graft_ratio = jnp.sqrt(grad_square + EPSILON) / jnp.sqrt(prec_square + EPSILON)
        return (preconditioned * graft_ratio).astype(jnp.bfloat16)
    updates = lax.map(precondition_block, (blocks, block_slot))
    return updates.reshape(MATS, NCB, KVW, B).transpose(0, 2, 1, 3).reshape(MATS, KVW, D)
```

```python
import functools
import jax
import jax.numpy as jnp
from jax import lax
from jax.experimental import pallas as pl
from jax.experimental.pallas import tpu as pltpu
from jax.sharding import PartitionSpec as P

EPSILON = 1e-06
LANES = 128
TERMS = 6
MIB = 1024 * 1024
VMEM_BYTES = 24 * MIB
bf16, f32 = jnp.bfloat16, jnp.float32

SELF, NEAR, FAR, OPPOSITE = range(4)


def masks(core):
    return 0, 1 + 2 * core, 3 - 2 * core, 2


def chip(place, relative):
    return lax.bitwise_xor(place[0] // 2, jnp.int32(masks(lax.rem(place[0], 2))[relative]))


def strip_columns(place, relative, core, j, width, strip):
    index = 2 * chip(place, relative) + core
    return pl.ds(pl.multiple_of(j * width + index * strip, strip), strip)


def together(copies):
    copies = list(copies)
    for copy in copies:
        copy.start()
    for copy in copies:
        copy.wait()


def strip_copies(place, grads_ref, out_ref, arrived, first, kinds, own, sizes):
    core = lax.rem(place[0], 2)
    core = core if own else 1 - core
    cols = sizes["cols"]
    order = (SELF, NEAR, FAR, OPPOSITE) if own else (SELF, FAR, NEAR, OPPOSITE)
    return [
        pltpu.make_async_copy(
            grads_ref.at[0, :, :, strip_columns(place, order[k], core, j, sizes["width"], sizes["strip"])],
            out_ref.at[n, :, j],
            arrived.at[first + n * cols + j],
        )
        for n, k in enumerate(kinds)
        for j in range(cols)
    ]


def send_kernel(place, grads_ref, send_ref, arrived, *, kinds, **sizes):
    together(strip_copies(place, grads_ref, send_ref, arrived, 0, kinds, False, sizes))


def send_and_keep_kernel(place, grads_ref, send_ref, keep_ref, arrived, *, kinds, kept, **sizes):
    together(
        strip_copies(place, grads_ref, send_ref, arrived, 0, kinds, False, sizes)
        + strip_copies(place, grads_ref, keep_ref, arrived, len(kinds) * sizes["cols"], kept, True, sizes)
    )


def pair_sum_kernel(keep_ref, got_ref, *sum_refs, first):
    for n, sum_ref in enumerate(sum_refs):
        sum_ref[...] = (keep_ref[first + n].astype(f32) + got_ref[n].astype(f32)).astype(bf16)


def add_kernel(x_ref, y_ref, out_ref):
    out_ref[...] = (x_ref[...].astype(f32) + y_ref[...].astype(f32)).astype(bf16)


def route_kernel(slot, *refs):
    *terms, out_ref = refs
    slots = out_ref.shape[1]
    cols = terms[0].shape[1]
    out_ref[...] = jnp.zeros_like(out_ref)
    for m in range(terms[0].shape[0]):
        for j in range(cols):
            q = slot[m * cols + j]
            total = sum(term[m, j].astype(f32) for term in terms)
            out_ref[q // slots, lax.rem(q, slots)] = total.astype(bf16)


def left_kernel(place, left_ref, block_ref, *out_refs):
    *half_refs, square_ref, scratch = out_refs
    owners, slots, rows, strip = block_ref.shape
    for s in range(slots):
        block = block_ref[:, s].reshape(owners * rows, strip)
        wide = block.astype(f32)
        square_ref[s] = jnp.broadcast_to(jnp.sum(wide * wide, keepdims=True), square_ref.shape[1:])
        half = jnp.dot(left_ref[s], block, preferred_element_type=f32)
        scratch[s] = half.reshape(scratch.shape[1:])
        for k, half_ref in enumerate(half_refs):
            half_ref[s] = scratch[s, :, chip(place, k)].reshape(half_ref.shape[1:]).astype(bf16)


def split3(x):
    a = x.astype(bf16).astype(f32)
    b = (x - a).astype(bf16).astype(f32)
    return a, b, x - a - b


def right_kernel(place, *refs):
    own_refs, twin_refs = refs[:4], refs[4:8]
    right_ref, square_ref, back_ref, half_scratch = refs[8:]
    owners, part, wide = back_ref.shape
    slots = right_ref.shape[0]
    width = (wide - LANES) // slots
    strip = own_refs[0].shape[2]
    core = lax.rem(place[0], 2)
    lane = lax.broadcasted_iota(jnp.int32, (part, LANES), 1)
    tail = jnp.zeros((part, LANES), f32)
    for s in range(slots):
        for half_refs, c in ((own_refs, core), (twin_refs, 1 - core)):
            for k, half_ref in enumerate(half_refs):
                r = 2 * chip(place, k) + c
                half_scratch[s, :, pl.ds(pl.multiple_of(r * strip, strip), strip)] = half_ref[s]
        columns = pl.ds(pl.multiple_of(core * width, width), width)
        prec = jnp.dot(half_scratch[s], right_ref[s, :, columns], preferred_element_type=f32)
        back_ref[:, :, s * width : (s + 1) * width] = prec.reshape(owners, part, width).astype(bf16)
        prec_square = jnp.broadcast_to(jnp.sum(prec * prec, keepdims=True), (part, LANES))
        for k, term in enumerate(split3(square_ref[s]) + split3(prec_square)):
            tail = jnp.where(lane == TERMS * s + k, term, tail)
    back_ref[:, :, slots * width :] = jnp.broadcast_to(tail[None], (owners, part, LANES)).astype(bf16)


def select_kernel(slot, back_ref, pair_ref):
    mats, count, part, wide = pair_ref.shape
    width = (wide - LANES) // 2
    lane = lax.broadcasted_iota(jnp.int32, (part, LANES), 1)
    for m in range(mats):
        for p in range(count):
            tails = []
            for h in range(2):
                q = slot[2 * (m * count + p) + h]
                s = lax.rem(q, 2)
                columns = pl.ds(pl.multiple_of(s * width, width), width)
                pair_ref[m, p, :, h * width : (h + 1) * width] = back_ref[q // 2, :, columns]
                tail = back_ref[q // 2, :, 2 * width :].astype(f32)
                tails.append(jnp.where(s == h, tail, pltpu.roll(tail, TERMS if h else LANES - TERMS, 1)))
            pair_ref[m, p, :, 2 * width :] = jnp.where(lane < TERMS, tails[0], tails[1]).astype(bf16)


def stack_kernel(*refs):
    *piece_refs, out_ref = refs
    for k, piece_ref in enumerate(piece_refs):
        out_ref[k] = piece_ref[...]


def finish_kernel(place, first_ref, second_ref, twin_first_ref, twin_second_ref, out_ref, ready, written, *, entries):
    _, mats, count, part, wide = first_ref.shape
    width = (wide - LANES) // 2
    lane = lax.broadcasted_iota(jnp.int32, (count, part, LANES), 2)

    def emit(m, own, twin, ratios, core, odd):
        couples = ((SELF, FAR), (OPPOSITE, NEAR)) if core else ((SELF, NEAR), (OPPOSITE, FAR))
        for couple in couples:
            rows = pl.ds(pl.multiple_of(chip(place, couple[0]) // 2 * 2 * part, 2 * part), 2 * part)
            for p in range(count):
                for h in range(2):
                    for pieces, c in ((own, core), (twin, 1 - core)):
                        tiles = [
                            pieces[k][p, :, h * width : (h + 1) * width].astype(f32) * ratios[h][p]
                            for k in (couple[::-1] if odd else couple)
                        ]
                        at = (2 * p + h) * 2 * width + c * width
                        ready[m, rows, pl.ds(at, width)] = jnp.concatenate(tiles, 0).astype(bf16)

    def write(m):
        return pltpu.make_async_copy(ready.at[m], out_ref.at[m], written.at[m])

    @pl.loop(0, mats)
    def _(m):
        own = [ref.at[n, m] for ref in (first_ref, second_ref) for n in range(2)]
        twin = [ref.at[n, m] for n in range(2) for ref in (twin_first_ref, twin_second_ref)]
        tail = sum(ref[:, :, 2 * width :].astype(f32) for ref in own + twin)
        ratios = []
        for h in range(2):
            terms = [
                jnp.sum(jnp.where((lane >= start) & (lane < start + 3), tail, 0.0), axis=2, keepdims=True)
                for start in (TERMS * h, TERMS * h + 3)
            ]
            ratios.append(jnp.sqrt(terms[0] / entries + EPSILON) / jnp.sqrt(terms[1] / entries + EPSILON))
        for core in range(2):
            for odd in range(2):
                here = (lax.rem(place[0], 2) == core) & (lax.rem(place[0] // 2, 2) == odd)
                pl.when(here)(functools.partial(emit, m, own, twin, ratios, core, odd))
        write(m).start()

    for m in range(mats):
        write(m).wait()


def on_device(grads, left_root, right_root, block_slot):
    owners = lax.axis_size("fsdp")
    reps = lax.axis_size("replica")
    slots, height, width = left_root.shape[0], left_root.shape[1], right_root.shape[1]
    _, mats, rows, full = grads.shape
    cols = full // width
    blocks = mats * cols
    strip = width // reps
    part = rows // 4
    shape = jax.ShapeDtypeStruct

    place = lax.axis_index("replica").reshape(1).astype(jnp.int32)
    def twin(x):
        return lax.ppermute(x, "replica", [(i, i ^ 1) for i in range(reps)])

    def exchange(x, relative):
        perm = [(i, i ^ (2 * masks(i % 2)[relative])) for i in range(reps)]
        return lax.ppermute(x, "replica", perm)

    sizes = dict(cols=cols, width=width, strip=strip)
    def strips(*n):
        return shape((*n, mats, cols, rows, strip), bf16)

    def local(kernel, in_specs, out_specs, out_shape, scratch_shapes=()):
        return pl.pallas_call(
            kernel,
            in_specs=in_specs,
            out_specs=out_specs,
            out_shape=out_shape,
            scratch_shapes=scratch_shapes,
            compiler_params=pltpu.CompilerParams(vmem_limit_bytes=VMEM_BYTES),
        )

    smem, vmem = pl.BlockSpec(memory_space=pltpu.SMEM), pl.BlockSpec(memory_space=pltpu.VMEM)
    hbm = pl.BlockSpec(memory_space=pl.ANY)
    in_hbm = pltpu.with_memory_space_constraint(grads, pltpu.HBM)
    ahead, behind = (OPPOSITE, NEAR), (SELF, FAR)
    send = local(
        functools.partial(send_kernel, kinds=ahead, **sizes),
        [smem, hbm],
        vmem,
        strips(2),
        [pltpu.SemaphoreType.DMA((2 * cols,))],
    )(place, in_hbm)
    got = twin(send)
    send, keep = local(
        functools.partial(send_and_keep_kernel, kinds=behind, kept=ahead + behind, **sizes),
        [smem, hbm],
        [vmem] * 2,
        [strips(2), strips(4)],
        [pltpu.SemaphoreType.DMA((6 * cols,))],
    )(place, in_hbm)
    got = (got, twin(send))
    sums = {}
    for n, kinds in enumerate((ahead, behind)):
        add = local(functools.partial(pair_sum_kernel, first=2 * n), [vmem] * 2, [vmem] * 2, [strips()] * 2)
        sums.update(zip(kinds, add(keep, got[n])))

    onward = exchange(sums[OPPOSITE], NEAR)
    direct = exchange(sums[NEAR], NEAR)
    passed = local(add_kernel, [vmem] * 2, vmem, strips())(sums[FAR], onward)
    last = exchange(passed, FAR)

    outgoing = local(route_kernel, [smem] + [vmem] * 3, vmem, shape((owners, slots, rows, strip), bf16))(
        block_slot, sums[SELF], direct, last
    )
    incoming = lax.all_to_all(outgoing, "fsdp", 0, 0, tiled=True)

    half_shape = shape((slots, owners * part, strip), bf16)
    *halves, square = local(
        left_kernel,
        [smem, vmem, vmem],
        [vmem] * 5,
        [half_shape] * 4 + [shape((slots, part, LANES), f32)],
        [pltpu.VMEM((slots, owners, 4, part, strip), f32)],
    )(place, left_root, incoming)
    halves = [halves[SELF]] + [exchange(halves[k], k) for k in (NEAR, FAR, OPPOSITE)]
    handed = [twin(half) for half in halves]
    handed = [handed[SELF], handed[FAR], handed[NEAR], handed[OPPOSITE]]
    wide = width + LANES
    back = local(
        right_kernel,
        [smem] + [vmem] * 10,
        vmem,
        shape((owners, part, wide), bf16),
        [pltpu.VMEM((slots, owners * part, width), bf16)],
    )(place, *halves, *handed, right_root, square)
    back = lax.all_to_all(back, "fsdp", 0, 0, tiled=True)

    count = cols // 2
    piece = (mats, count, part, wide)
    mine = local(select_kernel, [smem, vmem], vmem, shape(piece, bf16))(block_slot, back)
    near = exchange(mine, NEAR)
    first = local(stack_kernel, [vmem] * 2, vmem, shape((2, *piece), bf16))(mine, near)
    second = exchange(first, FAR)
    return local(
        functools.partial(finish_kernel, entries=height * width),
        [smem] + [vmem] * 4,
        pl.BlockSpec(memory_space=pl.ANY),
        shape((mats, rows, full), bf16),
        [pltpu.VMEM((mats, rows, full), bf16), pltpu.SemaphoreType.DMA((mats,))],
    )(place, first, second, twin(first), twin(second))


def solution(mesh):
    in_specs = (P("replica", None, "fsdp", None), P("fsdp", None, None), P("fsdp", None, None), P())
    return jax.shard_map(
        on_device, mesh=mesh, in_specs=in_specs, out_specs=P(None, "fsdp", None), check_vma=False
    )
```

```python
import functools
import jax
import jax.numpy as jnp
from jax import lax
from jax.experimental import pallas as pl
from jax.experimental.pallas import tpu as pltpu
from jax.sharding import PartitionSpec as P

EPSILON = 1e-06
LANES = 128
TERMS = 6
MIB = 1024 * 1024
VMEM_BYTES = 24 * MIB
bf16, f32 = jnp.bfloat16, jnp.float32

SELF, NEAR, FAR, OPPOSITE = range(4)


def masks(core):
    return 0, 1 + 2 * core, 3 - 2 * core, 2


def chip(place, relative):
    return lax.bitwise_xor(place[0] // 2, jnp.int32(masks(lax.rem(place[0], 2))[relative]))


def strip_columns(place, relative, core, j, width, strip):
    index = 2 * chip(place, relative) + core
    return pl.ds(pl.multiple_of(j * width + index * strip, strip), strip)


def together(copies):
    copies = list(copies)
    for copy in copies:
        copy.start()
    for copy in copies:
        copy.wait()


def send_kernel(place, grads_ref, send_ref, arrived, *, kinds, cols, width, strip):
    other = 1 - lax.rem(place[0], 2)
    order = (SELF, FAR, NEAR, OPPOSITE)
    together(
        pltpu.make_async_copy(
            grads_ref.at[0, :, :, strip_columns(place, order[k], other, j, width, strip)],
            send_ref.at[n, :, j],
            arrived.at[n * cols + j],
        )
        for n, k in enumerate(kinds)
        for j in range(cols)
    )


def pair_sum_kernel(place, grads_ref, got_ref, *sum_refs, kinds, cols, width, strip):
    core = lax.rem(place[0], 2)
    for n, (k, sum_ref) in enumerate(zip(kinds, sum_refs)):
        for m in range(grads_ref.shape[1]):
            for j in range(cols):
                piece = grads_ref[0, m, :, strip_columns(place, k, core, j, width, strip)]
                sum_ref[m, j] = (piece.astype(f32) + got_ref[n, m, j].astype(f32)).astype(bf16)


def add_kernel(x_ref, y_ref, out_ref):
    out_ref[...] = (x_ref[...].astype(f32) + y_ref[...].astype(f32)).astype(bf16)


def route_kernel(slot, *refs):
    *terms, out_ref = refs
    slots = out_ref.shape[1]
    cols = terms[0].shape[1]
    out_ref[...] = jnp.zeros_like(out_ref)
    for m in range(terms[0].shape[0]):
        for j in range(cols):
            q = slot[m * cols + j]
            total = sum(term[m, j].astype(f32) for term in terms)
            out_ref[q // slots, lax.rem(q, slots)] = total.astype(bf16)


def left_kernel(place, left_ref, block_ref, *out_refs):
    *half_refs, square_ref, scratch = out_refs
    owners, slots, rows, strip = block_ref.shape
    for s in range(slots):
        block = block_ref[:, s].reshape(owners * rows, strip)
        wide = block.astype(f32)
        square_ref[s] = jnp.broadcast_to(jnp.sum(wide * wide, keepdims=True), square_ref.shape[1:])
        half = jnp.dot(left_ref[s], block, preferred_element_type=f32)
        scratch[s] = half.reshape(scratch.shape[1:])
        for k, half_ref in enumerate(half_refs):
            half_ref[s] = scratch[s, :, chip(place, k)].reshape(half_ref.shape[1:]).astype(bf16)


def split3(x):
    a = x.astype(bf16).astype(f32)
    b = (x - a).astype(bf16).astype(f32)
    return a, b, x - a - b


def right_kernel(place, *refs):
    own_refs, twin_refs = refs[:4], refs[4:8]
    right_ref, square_ref, back_ref, half_scratch = refs[8:]
    owners, part, wide = back_ref.shape
    slots = right_ref.shape[0]
    width = (wide - LANES) // slots
    strip = own_refs[0].shape[2]
    core = lax.rem(place[0], 2)
    lane = lax.broadcasted_iota(jnp.int32, (part, LANES), 1)
    tail = jnp.zeros((part, LANES), f32)
    for s in range(slots):
        for half_refs, c in ((own_refs, core), (twin_refs, 1 - core)):
            for k, half_ref in enumerate(half_refs):
                r = 2 * chip(place, k) + c
                half_scratch[s, :, pl.ds(pl.multiple_of(r * strip, strip), strip)] = half_ref[s]
        columns = pl.ds(pl.multiple_of(core * width, width), width)
        prec = jnp.dot(half_scratch[s], right_ref[s, :, columns], preferred_element_type=f32)
        back_ref[:, :, s * width : (s + 1) * width] = prec.reshape(owners, part, width).astype(bf16)
        prec_square = jnp.broadcast_to(jnp.sum(prec * prec, keepdims=True), (part, LANES))
        for k, term in enumerate(split3(square_ref[s]) + split3(prec_square)):
            tail = jnp.where(lane == TERMS * s + k, term, tail)
    back_ref[:, :, slots * width :] = jnp.broadcast_to(tail[None], (owners, part, LANES)).astype(bf16)


def select_kernel(slot, back_ref, pair_ref):
    mats, count, part, wide = pair_ref.shape
    width = (wide - LANES) // 2
    lane = lax.broadcasted_iota(jnp.int32, (part, LANES), 1)
    for m in range(mats):
        for p in range(count):
            tails = []
            for h in range(2):
                q = slot[2 * (m * count + p) + h]
                s = lax.rem(q, 2)
                columns = pl.ds(pl.multiple_of(s * width, width), width)
                pair_ref[m, p, :, h * width : (h + 1) * width] = back_ref[q // 2, :, columns]
                tail = back_ref[q // 2, :, 2 * width :].astype(f32)
                tails.append(jnp.where(s == h, tail, pltpu.roll(tail, TERMS if h else LANES - TERMS, 1)))
            pair_ref[m, p, :, 2 * width :] = jnp.where(lane < TERMS, tails[0], tails[1]).astype(bf16)


def finish_kernel(place, *refs, entries):
    own_refs, twin_refs = refs[:4], refs[4:8]
    out_ref, ready, written = refs[8:]
    mats, count, part, wide = own_refs[0].shape
    width = (wide - LANES) // 2
    lane = lax.broadcasted_iota(jnp.int32, (count, part, LANES), 2)

    def emit(m, own, twin, ratios, core, odd):
        couples = ((SELF, FAR), (OPPOSITE, NEAR)) if core else ((SELF, NEAR), (OPPOSITE, FAR))
        for couple in couples:
            rows = pl.ds(pl.multiple_of(chip(place, couple[0]) // 2 * 2 * part, 2 * part), 2 * part)
            for p in range(count):
                for h in range(2):
                    for pieces, c in ((own, core), (twin, 1 - core)):
                        tiles = [
                            pieces[k][p, :, h * width : (h + 1) * width].astype(f32) * ratios[h][p]
                            for k in (couple[::-1] if odd else couple)
                        ]
                        at = (2 * p + h) * 2 * width + c * width
                        ready[m, rows, pl.ds(at, width)] = jnp.concatenate(tiles, 0).astype(bf16)

    def write(m):
        return pltpu.make_async_copy(ready.at[m], out_ref.at[m], written.at[m])

    @pl.loop(0, mats)
    def _(m):
        own = [ref.at[m] for ref in own_refs]
        twin = [ref.at[m] for ref in twin_refs]
        tail = sum(ref[:, :, 2 * width :].astype(f32) for ref in own + twin)
        ratios = []
        for h in range(2):
            terms = [
                jnp.sum(jnp.where((lane >= start) & (lane < start + 3), tail, 0.0), axis=2, keepdims=True)
                for start in (TERMS * h, TERMS * h + 3)
            ]
            ratios.append(jnp.sqrt(terms[0] / entries + EPSILON) / jnp.sqrt(terms[1] / entries + EPSILON))
        for core in range(2):
            for odd in range(2):
                here = (lax.rem(place[0], 2) == core) & (lax.rem(place[0] // 2, 2) == odd)
                pl.when(here)(functools.partial(emit, m, own, twin, ratios, core, odd))
        write(m).start()

    for m in range(mats):
        write(m).wait()


def on_device(grads, left_root, right_root, block_slot):
    owners = lax.axis_size("fsdp")
    reps = lax.axis_size("replica")
    slots, height, width = left_root.shape[0], left_root.shape[1], right_root.shape[1]
    _, mats, rows, full = grads.shape
    cols = full // width
    blocks = mats * cols
    strip = width // reps
    part = rows // 4
    shape = jax.ShapeDtypeStruct

    place = lax.axis_index("replica").reshape(1).astype(jnp.int32)
    def twin(x):
        return lax.ppermute(x, "replica", [(i, i ^ 1) for i in range(reps)])

    def exchange(x, relative):
        perm = [(i, i ^ (2 * masks(i % 2)[relative])) for i in range(reps)]
        return lax.ppermute(x, "replica", perm)

    sizes = dict(cols=cols, width=width, strip=strip)
    def strips(*n):
        return shape((*n, mats, cols, rows, strip), bf16)

    def local(kernel, in_specs, out_specs, out_shape, scratch_shapes=()):
        return pl.pallas_call(
            kernel,
            in_specs=in_specs,
            out_specs=out_specs,
            out_shape=out_shape,
            scratch_shapes=scratch_shapes,
            compiler_params=pltpu.CompilerParams(vmem_limit_bytes=VMEM_BYTES),
        )

    smem, vmem = pl.BlockSpec(memory_space=pltpu.SMEM), pl.BlockSpec(memory_space=pltpu.VMEM)
    sums = {}
    for kinds in ((OPPOSITE, NEAR), (SELF, FAR)):
        send = local(
            functools.partial(send_kernel, kinds=kinds, **sizes),
            [smem, pl.BlockSpec(memory_space=pl.ANY)],
            vmem,
            strips(2),
            [pltpu.SemaphoreType.DMA((2 * cols,))],
        )(place, pltpu.with_memory_space_constraint(grads, pltpu.HBM))
        got = twin(send)
        found = local(
            functools.partial(pair_sum_kernel, kinds=kinds, **sizes), [smem, vmem, vmem], [vmem] * 2, [strips()] * 2
        )(place, grads, got)
        sums.update(zip(kinds, found))

    onward = exchange(sums[OPPOSITE], NEAR)
    direct = exchange(sums[NEAR], NEAR)
    passed = local(add_kernel, [vmem] * 2, vmem, strips())(sums[FAR], onward)
    last = exchange(passed, FAR)

    outgoing = local(route_kernel, [smem] + [vmem] * 3, vmem, shape((owners, slots, rows, strip), bf16))(
        block_slot, sums[SELF], direct, last
    )
    incoming = lax.all_to_all(outgoing, "fsdp", 0, 0, tiled=True)

    half_shape = shape((slots, owners * part, strip), bf16)
    *halves, square = local(
        left_kernel,
        [smem, vmem, vmem],
        [vmem] * 5,
        [half_shape] * 4 + [shape((slots, part, LANES), f32)],
        [pltpu.VMEM((slots, owners, 4, part, strip), f32)],
    )(place, left_root, incoming)
    halves = [halves[SELF]] + [exchange(halves[k], k) for k in (NEAR, FAR, OPPOSITE)]
    handed = [twin(half) for half in halves]
    handed = [handed[SELF], handed[FAR], handed[NEAR], handed[OPPOSITE]]
    wide = width + LANES
    back = local(
        right_kernel,
        [smem] + [vmem] * 10,
        vmem,
        shape((owners, part, wide), bf16),
        [pltpu.VMEM((slots, owners * part, width), bf16)],
    )(place, *halves, *handed, right_root, square)
    back = lax.all_to_all(back, "fsdp", 0, 0, tiled=True)

    count = cols // 2
    piece = (mats, count, part, wide)
    mine = local(select_kernel, [smem, vmem], vmem, shape(piece, bf16))(block_slot, back)
    near = exchange(mine, NEAR)
    far = exchange(mine, FAR)
    opposite = exchange(near, FAR)
    own = [mine, near, far, opposite]
    other = [twin(x) for x in (mine, far, near, opposite)]
    return local(
        functools.partial(finish_kernel, entries=height * width),
        [smem] + [vmem] * 8,
        pl.BlockSpec(memory_space=pl.ANY),
        shape((mats, rows, full), bf16),
        [pltpu.VMEM((mats, rows, full), bf16), pltpu.SemaphoreType.DMA((mats,))],
    )(place, *own, *other)


def solution(mesh):
    in_specs = (P("replica", None, "fsdp", None), P("fsdp", None, None), P("fsdp", None, None), P())
    return jax.shard_map(
        on_device, mesh=mesh, in_specs=in_specs, out_specs=P(None, "fsdp", None), check_vma=False
    )
```

```python
import functools
import jax
import jax.numpy as jnp
from jax import lax
from jax.experimental import pallas as pl
from jax.experimental.pallas import tpu as pltpu
from jax.sharding import PartitionSpec as P

EPSILON = 1e-06
LANES = 128
TERMS = 6
MIB = 1024 * 1024
VMEM_BYTES = 24 * MIB
bf16, f32 = jnp.bfloat16, jnp.float32

SELF, NEAR, FAR, OPPOSITE = range(4)
ORDER = (SELF, OPPOSITE, NEAR, FAR)
TWIN_ORDER = (SELF, OPPOSITE, FAR, NEAR)


def masks(core):
    return 0, 3 - 2 * core, 1 + 2 * core, 2


def chip(place, relative):
    return lax.bitwise_xor(place[0] // 2, jnp.int32(masks(lax.rem(place[0], 2))[relative]))


def strip_columns(place, relative, core, j, width, strip):
    index = 2 * chip(place, relative) + core
    return pl.ds(pl.multiple_of(j * width + index * strip, strip), strip)


def together(copies):
    copies = list(copies)
    for copy in copies:
        copy.start()
    for copy in copies:
        copy.wait()


def send_kernel(place, grads_ref, send_ref, arrived, *, kinds, cols, width, strip):
    other = 1 - lax.rem(place[0], 2)
    order = (SELF, FAR, NEAR, OPPOSITE)
    together(
        pltpu.make_async_copy(
            grads_ref.at[0, :, :, strip_columns(place, order[k], other, j, width, strip)],
            send_ref.at[n, :, j],
            arrived.at[n * cols + j],
        )
        for n, k in enumerate(kinds)
        for j in range(cols)
    )


def pair_sum_kernel(place, grads_ref, got_ref, *sum_refs, kinds, cols, width, strip):
    core = lax.rem(place[0], 2)
    for n, (k, sum_ref) in enumerate(zip(kinds, sum_refs)):
        for m in range(grads_ref.shape[1]):
            for j in range(cols):
                piece = grads_ref[0, m, :, strip_columns(place, k, core, j, width, strip)]
                sum_ref[m, j] = (piece.astype(f32) + got_ref[n, m, j].astype(f32)).astype(bf16)


def add_kernel(x_ref, y_ref, out_ref):
    out_ref[...] = (x_ref[...].astype(f32) + y_ref[...].astype(f32)).astype(bf16)


def route_kernel(slot, *refs):
    *terms, out_ref = refs
    slots = out_ref.shape[1]
    cols = terms[0].shape[1]
    out_ref[...] = jnp.zeros_like(out_ref)
    for m in range(terms[0].shape[0]):
        for j in range(cols):
            q = slot[m * cols + j]
            total = sum(term[m, j].astype(f32) for term in terms)
            out_ref[q // slots, lax.rem(q, slots)] = total.astype(bf16)


def left_kernel(place, left_ref, block_ref, *out_refs):
    *half_refs, square_ref, scratch = out_refs
    owners, slots, rows, strip = block_ref.shape
    for s in range(slots):
        block = block_ref[:, s].reshape(owners * rows, strip)
        wide = block.astype(f32)
        square_ref[s] = jnp.broadcast_to(jnp.sum(wide * wide, keepdims=True), square_ref.shape[1:])
        half = jnp.dot(left_ref[s], block, preferred_element_type=f32)
        scratch[s] = half.reshape(scratch.shape[1:])
        for k, half_ref in zip(ORDER, half_refs):
            half_ref[s] = scratch[s, :, chip(place, k)].reshape(half_ref.shape[1:]).astype(bf16)


def split3(x):
    a = x.astype(bf16).astype(f32)
    b = (x - a).astype(bf16).astype(f32)
    return a, b, x - a - b


def right_kernel(place, *refs):
    own_refs, twin_refs = refs[:4], refs[4:8]
    right_ref, square_ref, back_ref, half_scratch = refs[8:]
    owners, part, wide = back_ref.shape
    slots = right_ref.shape[0]
    width = (wide - LANES) // slots
    strip = own_refs[0].shape[2]
    core = lax.rem(place[0], 2)
    lane = lax.broadcasted_iota(jnp.int32, (part, LANES), 1)
    tail = jnp.zeros((part, LANES), f32)
    for s in range(slots):
        for half_refs, c in ((own_refs, core), (twin_refs, 1 - core)):
            for k, half_ref in zip(ORDER, half_refs):
                r = 2 * chip(place, k) + c
                half_scratch[s, :, pl.ds(pl.multiple_of(r * strip, strip), strip)] = half_ref[s]
        columns = pl.ds(pl.multiple_of(core * width, width), width)
        prec = jnp.dot(half_scratch[s], right_ref[s, :, columns], preferred_element_type=f32)
        back_ref[:, :, s * width : (s + 1) * width] = prec.reshape(owners, part, width).astype(bf16)
        prec_square = jnp.broadcast_to(jnp.sum(prec * prec, keepdims=True), (part, LANES))
        for k, term in enumerate(split3(square_ref[s]) + split3(prec_square)):
            tail = jnp.where(lane == TERMS * s + k, term, tail)
    back_ref[:, :, slots * width :] = jnp.broadcast_to(tail[None], (owners, part, LANES)).astype(bf16)


def select_kernel(slot, back_ref, pair_ref):
    mats, count, part, wide = pair_ref.shape
    width = (wide - LANES) // 2
    lane = lax.broadcasted_iota(jnp.int32, (part, LANES), 1)
    for m in range(mats):
        for p in range(count):
            tails = []
            for h in range(2):
                q = slot[2 * (m * count + p) + h]
                s = lax.rem(q, 2)
                columns = pl.ds(pl.multiple_of(s * width, width), width)
                pair_ref[m, p, :, h * width : (h + 1) * width] = back_ref[q // 2, :, columns]
                tail = back_ref[q // 2, :, 2 * width :].astype(f32)
                tails.append(jnp.where(s == h, tail, pltpu.roll(tail, TERMS if h else LANES - TERMS, 1)))
            pair_ref[m, p, :, 2 * width :] = jnp.where(lane < TERMS, tails[0], tails[1]).astype(bf16)


def finish_kernel(place, *refs, entries):
    own_refs, twin_refs = refs[:4], refs[4:8]
    out_ref, ready, written = refs[8:]
    mats, count, part, wide = own_refs[0].shape
    width = (wide - LANES) // 2
    lane = lax.broadcasted_iota(jnp.int32, (count, part, LANES), 2)

    def emit(m, own, twin, ratios, core, odd):
        couples = ((SELF, NEAR), (OPPOSITE, FAR)) if core else ((SELF, FAR), (OPPOSITE, NEAR))
        for couple in couples:
            rows = pl.ds(pl.multiple_of(chip(place, couple[0]) // 2 * 2 * part, 2 * part), 2 * part)
            for p in range(count):
                for h in range(2):
                    for pieces, c in ((own, core), (twin, 1 - core)):
                        tiles = [
                            pieces[k][p, :, h * width : (h + 1) * width].astype(f32) * ratios[h][p]
                            for k in (couple[::-1] if odd else couple)
                        ]
                        at = (2 * p + h) * 2 * width + c * width
                        ready[m, rows, pl.ds(at, width)] = jnp.concatenate(tiles, 0).astype(bf16)

    def write(m):
        return pltpu.make_async_copy(ready.at[m], out_ref.at[m], written.at[m])

    @pl.loop(0, mats)
    def _(m):
        own = [ref.at[m] for ref in own_refs]
        twin = [ref.at[m] for ref in twin_refs]
        tail = sum(ref[:, :, 2 * width :].astype(f32) for ref in own + twin)
        ratios = []
        for h in range(2):
            terms = [
                jnp.sum(jnp.where((lane >= start) & (lane < start + 3), tail, 0.0), axis=2, keepdims=True)
                for start in (TERMS * h, TERMS * h + 3)
            ]
            ratios.append(jnp.sqrt(terms[0] / entries + EPSILON) / jnp.sqrt(terms[1] / entries + EPSILON))
        for core in range(2):
            for odd in range(2):
                here = (lax.rem(place[0], 2) == core) & (lax.rem(place[0] // 2, 2) == odd)
                pl.when(here)(functools.partial(emit, m, own, twin, ratios, core, odd))
        write(m).start()

    for m in range(mats):
        write(m).wait()


def on_device(grads, left_root, right_root, block_slot):
    owners = lax.axis_size("fsdp")
    reps = lax.axis_size("replica")
    slots, height, width = left_root.shape[0], left_root.shape[1], right_root.shape[1]
    _, mats, rows, full = grads.shape
    cols = full // width
    blocks = mats * cols
    strip = width // reps
    part = rows // 4
    shape = jax.ShapeDtypeStruct

    place = lax.axis_index("replica").reshape(1).astype(jnp.int32)
    def twin(x):
        return lax.ppermute(x, "replica", [(i, i ^ 1) for i in range(reps)])

    def exchange(x, relative):
        perm = [(i, i ^ (2 * masks(i % 2)[relative])) for i in range(reps)]
        return lax.ppermute(x, "replica", perm)

    sizes = dict(cols=cols, width=width, strip=strip)
    def strips(*n):
        return shape((*n, mats, cols, rows, strip), bf16)

    def local(kernel, in_specs, out_specs, out_shape, scratch_shapes=()):
        return pl.pallas_call(
            kernel,
            in_specs=in_specs,
            out_specs=out_specs,
            out_shape=out_shape,
            scratch_shapes=scratch_shapes,
            compiler_params=pltpu.CompilerParams(vmem_limit_bytes=VMEM_BYTES),
        )

    smem, vmem = pl.BlockSpec(memory_space=pltpu.SMEM), pl.BlockSpec(memory_space=pltpu.VMEM)
    sums = {}
    for kinds in ((OPPOSITE, NEAR), (SELF, FAR)):
        send = local(
            functools.partial(send_kernel, kinds=kinds, **sizes),
            [smem, pl.BlockSpec(memory_space=pl.ANY)],
            vmem,
            strips(2),
            [pltpu.SemaphoreType.DMA((2 * cols,))],
        )(place, pltpu.with_memory_space_constraint(grads, pltpu.HBM))
        got = twin(send)
        found = local(
            functools.partial(pair_sum_kernel, kinds=kinds, **sizes), [smem, vmem, vmem], [vmem] * 2, [strips()] * 2
        )(place, grads, got)
        sums.update(zip(kinds, found))

    onward = exchange(sums[OPPOSITE], NEAR)
    direct = exchange(sums[NEAR], NEAR)
    passed = local(add_kernel, [vmem] * 2, vmem, strips())(sums[FAR], onward)
    last = exchange(passed, FAR)

    outgoing = local(route_kernel, [smem] + [vmem] * 3, vmem, shape((owners, slots, rows, strip), bf16))(
        block_slot, sums[SELF], direct, last
    )
    incoming = lax.all_to_all(outgoing, "fsdp", 0, 0, tiled=True)

    half_shape = shape((slots, owners * part, strip), bf16)
    *halves, square = local(
        left_kernel,
        [smem, vmem, vmem],
        [vmem] * 5,
        [half_shape] * 4 + [shape((slots, part, LANES), f32)],
        [pltpu.VMEM((slots, owners, 4, part, strip), f32)],
    )(place, left_root, incoming)
    halves = [half if k == SELF else exchange(half, k) for k, half in zip(ORDER, halves)]
    handed = [twin(halves[ORDER.index(k)]) for k in TWIN_ORDER]
    wide = width + LANES
    back = local(
        right_kernel,
        [smem] + [vmem] * 10,
        vmem,
        shape((owners, part, wide), bf16),
        [pltpu.VMEM((slots, owners * part, width), bf16)],
    )(place, *halves, *handed, right_root, square)
    back = lax.all_to_all(back, "fsdp", 0, 0, tiled=True)

    count = cols // 2
    piece = (mats, count, part, wide)
    mine = local(select_kernel, [smem, vmem], vmem, shape(piece, bf16))(block_slot, back)
    near = exchange(mine, NEAR)
    shared = twin(mine)
    later, shared = lax.optimization_barrier((mine, shared))
    far = exchange(later, FAR)
    opposite = exchange(near, FAR)
    own = [mine, near, far, opposite]
    other = [shared] + [twin(x) for x in (far, near, opposite)]
    return local(
        functools.partial(finish_kernel, entries=height * width),
        [smem] + [vmem] * 8,
        pl.BlockSpec(memory_space=pl.ANY),
        shape((mats, rows, full), bf16),
        [pltpu.VMEM((mats, rows, full), bf16), pltpu.SemaphoreType.DMA((mats,))],
    )(place, *own, *other)


def solution(mesh):
    in_specs = (P("replica", None, "fsdp", None), P("fsdp", None, None), P("fsdp", None, None), P())
    return jax.shard_map(
        on_device, mesh=mesh, in_specs=in_specs, out_specs=P(None, "fsdp", None), check_vma=False
    )
```

```python
import functools
import jax
import jax.numpy as jnp
from jax import lax
from jax.experimental import pallas as pl
from jax.experimental.pallas import tpu as pltpu
from jax.sharding import PartitionSpec as P

EPSILON = 1e-06
LANES = 128
TERMS = 6
MIB = 1024 * 1024
VMEM_BYTES = 24 * MIB
bf16, f32 = jnp.bfloat16, jnp.float32

SELF, NEAR, FAR, OPPOSITE = range(4)
ORDER = (SELF, OPPOSITE, NEAR, FAR)
TWIN_ORDER = (SELF, OPPOSITE, FAR, NEAR)


def masks(core):
    return 0, 1 + 2 * core, 3 - 2 * core, 2


def chip(place, relative):
    return lax.bitwise_xor(place[0] // 2, jnp.int32(masks(lax.rem(place[0], 2))[relative]))


def strip_columns(place, relative, core, j, width, strip):
    index = 2 * chip(place, relative) + core
    return pl.ds(pl.multiple_of(j * width + index * strip, strip), strip)


def together(copies):
    copies = list(copies)
    for copy in copies:
        copy.start()
    for copy in copies:
        copy.wait()


def send_kernel(place, grads_ref, send_ref, arrived, *, kinds, cols, width, strip):
    other = 1 - lax.rem(place[0], 2)
    order = (SELF, FAR, NEAR, OPPOSITE)
    together(
        pltpu.make_async_copy(
            grads_ref.at[0, :, :, strip_columns(place, order[k], other, j, width, strip)],
            send_ref.at[n, :, j],
            arrived.at[n * cols + j],
        )
        for n, k in enumerate(kinds)
        for j in range(cols)
    )


def pair_sum_kernel(place, grads_ref, got_ref, *sum_refs, kinds, cols, width, strip):
    core = lax.rem(place[0], 2)
    for n, (k, sum_ref) in enumerate(zip(kinds, sum_refs)):
        for m in range(grads_ref.shape[1]):
            for j in range(cols):
                piece = grads_ref[0, m, :, strip_columns(place, k, core, j, width, strip)]
                sum_ref[m, j] = (piece.astype(f32) + got_ref[n, m, j].astype(f32)).astype(bf16)


def add_kernel(x_ref, y_ref, out_ref):
    out_ref[...] = (x_ref[...].astype(f32) + y_ref[...].astype(f32)).astype(bf16)


def route_kernel(slot, *refs):
    *terms, out_ref = refs
    slots = out_ref.shape[1]
    cols = terms[0].shape[1]
    out_ref[...] = jnp.zeros_like(out_ref)
    for m in range(terms[0].shape[0]):
        for j in range(cols):
            q = slot[m * cols + j]
            total = sum(term[m, j].astype(f32) for term in terms)
            out_ref[q // slots, lax.rem(q, slots)] = total.astype(bf16)


def left_kernel(place, left_ref, block_ref, *out_refs):
    *half_refs, square_ref, scratch = out_refs
    owners, slots, rows, strip = block_ref.shape
    for s in range(slots):
        block = block_ref[:, s].reshape(owners * rows, strip)
        wide = block.astype(f32)
        square_ref[s] = jnp.broadcast_to(jnp.sum(wide * wide, keepdims=True), square_ref.shape[1:])
        half = jnp.dot(left_ref[s], block, preferred_element_type=f32)
        scratch[s] = half.reshape(scratch.shape[1:])
        for k, half_ref in zip(ORDER, half_refs):
            half_ref[s] = scratch[s, :, chip(place, k)].reshape(half_ref.shape[1:]).astype(bf16)


def split3(x):
    a = x.astype(bf16).astype(f32)
    b = (x - a).astype(bf16).astype(f32)
    return a, b, x - a - b


def right_kernel(place, *refs):
    own_refs, twin_refs = refs[:4], refs[4:8]
    right_ref, square_ref, back_ref, half_scratch = refs[8:]
    owners, part, wide = back_ref.shape
    slots = right_ref.shape[0]
    width = (wide - LANES) // slots
    strip = own_refs[0].shape[2]
    core = lax.rem(place[0], 2)
    lane = lax.broadcasted_iota(jnp.int32, (part, LANES), 1)
    tail = jnp.zeros((part, LANES), f32)
    for s in range(slots):
        for half_refs, c in ((own_refs, core), (twin_refs, 1 - core)):
            for k, half_ref in zip(ORDER, half_refs):
                r = 2 * chip(place, k) + c
                half_scratch[s, :, pl.ds(pl.multiple_of(r * strip, strip), strip)] = half_ref[s]
        columns = pl.ds(pl.multiple_of(core * width, width), width)
        prec = jnp.dot(half_scratch[s], right_ref[s, :, columns], preferred_element_type=f32)
        back_ref[:, :, s * width : (s + 1) * width] = prec.reshape(owners, part, width).astype(bf16)
        prec_square = jnp.broadcast_to(jnp.sum(prec * prec, keepdims=True), (part, LANES))
        for k, term in enumerate(split3(square_ref[s]) + split3(prec_square)):
            tail = jnp.where(lane == TERMS * s + k, term, tail)
    back_ref[:, :, slots * width :] = jnp.broadcast_to(tail[None], (owners, part, LANES)).astype(bf16)


def select_kernel(slot, back_ref, tiles_ref):
    part, wide = back_ref.shape[1:]
    width = (wide - LANES) // 2
    each = width // LANES
    blocks = (tiles_ref.shape[0] - 2) // each
    lane = lax.broadcasted_iota(jnp.int32, (part, LANES), 1)
    line = lax.broadcasted_iota(jnp.int32, (part, LANES), 0)
    terms = [jnp.zeros((part, LANES), f32)] * 2
    for b in range(blocks):
        q, h, pair = slot[b], b % 2, b // 2
        s = lax.rem(q, 2)
        for t in range(each):
            columns = pl.ds(pl.multiple_of(s * width + t * LANES, LANES), LANES)
            tiles_ref[b * each + t] = back_ref[q // 2, :, columns]
        tail = back_ref[q // 2, :, 2 * width :].astype(f32)
        tail = jnp.where(s == h, tail, pltpu.roll(tail, TERMS if h else LANES - TERMS, 1))
        here = (line == pair % part) & (lane >= TERMS * h) & (lane < TERMS * (h + 1))
        terms[pair // part] = jnp.where(here, tail, terms[pair // part])
    for n in range(2):
        tiles_ref[blocks * each + n] = terms[n].astype(bf16)


def finish_kernel(place, *refs, entries):
    own_refs, twin_refs = refs[:4], refs[4:8]
    out_ref, ready, ratios, written = refs[8:]
    part = own_refs[0].shape[1]
    mats, rows, full = ready.shape
    blocks = ratios.shape[0]
    each = (own_refs[0].shape[0] - 2) // blocks
    count = blocks // mats
    lane = lax.broadcasted_iota(jnp.int32, (part, LANES), 1)
    for n in range(2):
        tail = sum(ref[blocks * each + n].astype(f32) for ref in own_refs + twin_refs)
        for h in range(2):
            block_square, prec_square = [
                jnp.sum(jnp.where((lane >= start) & (lane < start + 3), tail, 0.0), axis=1, keepdims=True)
                for start in (TERMS * h, TERMS * h + 3)
            ]
            ratio = jnp.sqrt(block_square / entries + EPSILON) / jnp.sqrt(prec_square / entries + EPSILON)
            for line in range(part):
                ratios[2 * (n * part + line) + h] = jnp.broadcast_to(ratio[line : line + 1], (part, LANES))

    def emit(m, core, odd):
        couples = ((SELF, FAR), (OPPOSITE, NEAR)) if core else ((SELF, NEAR), (OPPOSITE, FAR))
        for couple in couples:
            at = pl.ds(pl.multiple_of(chip(place, couple[0]) // 2 * 2 * part, 2 * part), 2 * part)
            for j in range(count):
                b = m * count + j
                for refs, c in ((own_refs, core), (twin_refs, 1 - core)):
                    for t in range(each):
                        tiles = [
                            refs[k][b * each + t].astype(f32) * ratios[b] for k in (couple[::-1] if odd else couple)
                        ]
                        columns = pl.ds(((2 * j + c) * each + t) * LANES, LANES)
                        ready[m, at, columns] = jnp.concatenate(tiles, 0).astype(bf16)

    def write(m):
        return pltpu.make_async_copy(ready.at[m], out_ref.at[m], written.at[m])

    @pl.loop(0, mats)
    def _(m):
        for core in range(2):
            for odd in range(2):
                here = (lax.rem(place[0], 2) == core) & (lax.rem(place[0] // 2, 2) == odd)
                pl.when(here)(functools.partial(emit, m, core, odd))
        write(m).start()

    for m in range(mats):
        write(m).wait()


def on_device(grads, left_root, right_root, block_slot):
    owners = lax.axis_size("fsdp")
    reps = lax.axis_size("replica")
    slots, height, width = left_root.shape[0], left_root.shape[1], right_root.shape[1]
    _, mats, rows, full = grads.shape
    cols = full // width
    blocks = mats * cols
    strip = width // reps
    part = rows // 4
    shape = jax.ShapeDtypeStruct

    place = lax.axis_index("replica").reshape(1).astype(jnp.int32)
    def twin(x):
        return lax.ppermute(x, "replica", [(i, i ^ 1) for i in range(reps)])

    def exchange(x, relative):
        perm = [(i, i ^ (2 * masks(i % 2)[relative])) for i in range(reps)]
        return lax.ppermute(x, "replica", perm)

    sizes = dict(cols=cols, width=width, strip=strip)
    def strips(*n):
        return shape((*n, mats, cols, rows, strip), bf16)

    def local(kernel, in_specs, out_specs, out_shape, scratch_shapes=()):
        return pl.pallas_call(
            kernel,
            in_specs=in_specs,
            out_specs=out_specs,
            out_shape=out_shape,
            scratch_shapes=scratch_shapes,
            compiler_params=pltpu.CompilerParams(vmem_limit_bytes=VMEM_BYTES),
        )

    smem, vmem = pl.BlockSpec(memory_space=pltpu.SMEM), pl.BlockSpec(memory_space=pltpu.VMEM)
    sums = {}
    for kinds in ((OPPOSITE, NEAR), (SELF, FAR)):
        send = local(
            functools.partial(send_kernel, kinds=kinds, **sizes),
            [smem, pl.BlockSpec(memory_space=pl.ANY)],
            vmem,
            strips(2),
            [pltpu.SemaphoreType.DMA((2 * cols,))],
        )(place, pltpu.with_memory_space_constraint(grads, pltpu.HBM))
        got = twin(send)
        found = local(
            functools.partial(pair_sum_kernel, kinds=kinds, **sizes), [smem, vmem, vmem], [vmem] * 2, [strips()] * 2
        )(place, grads, got)
        sums.update(zip(kinds, found))

    onward = exchange(sums[OPPOSITE], NEAR)
    direct = exchange(sums[NEAR], NEAR)
    passed = local(add_kernel, [vmem] * 2, vmem, strips())(sums[FAR], onward)
    last = exchange(passed, FAR)

    outgoing = local(route_kernel, [smem] + [vmem] * 3, vmem, shape((owners, slots, rows, strip), bf16))(
        block_slot, sums[SELF], direct, last
    )
    incoming = lax.all_to_all(outgoing, "fsdp", 0, 0, tiled=True)

    half_shape = shape((slots, owners * part, strip), bf16)
    *halves, square = local(
        left_kernel,
        [smem, vmem, vmem],
        [vmem] * 5,
        [half_shape] * 4 + [shape((slots, part, LANES), f32)],
        [pltpu.VMEM((slots, owners, 4, part, strip), f32)],
    )(place, left_root, incoming)
    halves = [half if k == SELF else exchange(half, k) for k, half in zip(ORDER, halves)]
    handed = [twin(halves[ORDER.index(k)]) for k in TWIN_ORDER]
    wide = width + LANES
    back = local(
        right_kernel,
        [smem] + [vmem] * 10,
        vmem,
        shape((owners, part, wide), bf16),
        [pltpu.VMEM((slots, owners * part, width), bf16)],
    )(place, *halves, *handed, right_root, square)
    back = lax.all_to_all(back, "fsdp", 0, 0, tiled=True)

    tiles = blocks * (width // 2 // LANES) + 2
    mine = local(select_kernel, [smem, vmem], vmem, shape((tiles, part, LANES), bf16))(block_slot, back)
    near = exchange(mine, NEAR)
    far = exchange(mine, FAR)
    opposite = exchange(near, FAR)
    own = [mine, near, far, opposite]
    other = [twin(x) for x in (mine, far, near, opposite)]
    return local(
        functools.partial(finish_kernel, entries=height * width),
        [smem] + [vmem] * 8,
        pl.BlockSpec(memory_space=pl.ANY),
        shape((mats, rows, full), bf16),
        [
            pltpu.VMEM((mats, rows, full), bf16),
            pltpu.VMEM((blocks, part, LANES), f32),
            pltpu.SemaphoreType.DMA((mats,)),
        ],
    )(place, *own, *other)


def solution(mesh):
    in_specs = (P("replica", None, "fsdp", None), P("fsdp", None, None), P("fsdp", None, None), P())
    return jax.shard_map(
        on_device, mesh=mesh, in_specs=in_specs, out_specs=P(None, "fsdp", None), check_vma=False
    )
```

```python
import functools
import jax
import jax.numpy as jnp
from jax import lax
from jax.experimental import pallas as pl
from jax.experimental.pallas import tpu as pltpu
from jax.sharding import PartitionSpec as P

EPSILON = 1e-06
LANES = 128
TERMS = 6
MIB = 1024 * 1024
VMEM_BYTES = 24 * MIB
bf16, f32 = jnp.bfloat16, jnp.float32

SELF, NEAR, FAR, OPPOSITE = range(4)
ORDER = (SELF, OPPOSITE, NEAR, FAR)
TWIN_ORDER = (SELF, OPPOSITE, FAR, NEAR)


def masks(core):
    return 0, 1 + 2 * core, 3 - 2 * core, 2


def chip(place, relative):
    return lax.bitwise_xor(place[0] // 2, jnp.int32(masks(lax.rem(place[0], 2))[relative]))


def strip_columns(place, relative, core, j, width, strip):
    index = 2 * chip(place, relative) + core
    return pl.ds(pl.multiple_of(j * width + index * strip, strip), strip)


def together(copies):
    copies = list(copies)
    for copy in copies:
        copy.start()
    for copy in copies:
        copy.wait()


def send_kernel(place, grads_ref, send_ref, arrived, *, kinds, cols, width, strip):
    other = 1 - lax.rem(place[0], 2)
    order = (SELF, FAR, NEAR, OPPOSITE)
    together(
        pltpu.make_async_copy(
            grads_ref.at[0, :, :, strip_columns(place, order[k], other, j, width, strip)],
            send_ref.at[n, :, j],
            arrived.at[n * cols + j],
        )
        for n, k in enumerate(kinds)
        for j in range(cols)
    )


def pair_sum_kernel(place, grads_ref, got_ref, *sum_refs, kinds, cols, width, strip):
    core = lax.rem(place[0], 2)
    for n, (k, sum_ref) in enumerate(zip(kinds, sum_refs)):
        for m in range(grads_ref.shape[1]):
            for j in range(cols):
                piece = grads_ref[0, m, :, strip_columns(place, k, core, j, width, strip)]
                sum_ref[m, j] = (piece.astype(f32) + got_ref[n, m, j].astype(f32)).astype(bf16)


def add_kernel(x_ref, y_ref, out_ref):
    out_ref[...] = (x_ref[...].astype(f32) + y_ref[...].astype(f32)).astype(bf16)


def route_kernel(slot, *refs):
    *terms, out_ref = refs
    slots = out_ref.shape[1]
    cols = terms[0].shape[1]
    out_ref[...] = jnp.zeros_like(out_ref)
    for m in range(terms[0].shape[0]):
        for j in range(cols):
            q = slot[m * cols + j]
            total = sum(term[m, j].astype(f32) for term in terms)
            out_ref[q // slots, lax.rem(q, slots)] = total.astype(bf16)


def left_kernel(place, left_ref, block_ref, *out_refs):
    *half_refs, square_ref, scratch = out_refs
    owners, slots, rows, strip = block_ref.shape
    for s in range(slots):
        block = block_ref[:, s].reshape(owners * rows, strip)
        wide = block.astype(f32)
        square_ref[s] = jnp.broadcast_to(jnp.sum(wide * wide, keepdims=True), square_ref.shape[1:])
        half = jnp.dot(left_ref[s], block, preferred_element_type=f32)
        scratch[s] = half.reshape(scratch.shape[1:])
        for k, half_ref in zip(ORDER, half_refs):
            half_ref[s] = scratch[s, :, chip(place, k)].reshape(half_ref.shape[1:]).astype(bf16)


def split3(x):
    a = x.astype(bf16).astype(f32)
    b = (x - a).astype(bf16).astype(f32)
    return a, b, x - a - b


def right_kernel(place, *refs):
    own_refs, twin_refs = refs[:4], refs[4:8]
    right_ref, square_ref, back_ref, half_scratch = refs[8:]
    owners, part, wide = back_ref.shape
    slots = right_ref.shape[0]
    width = (wide - LANES) // slots
    strip = own_refs[0].shape[2]
    core = lax.rem(place[0], 2)
    lane = lax.broadcasted_iota(jnp.int32, (part, LANES), 1)
    tail = jnp.zeros((part, LANES), f32)
    for s in range(slots):
        for half_refs, c in ((own_refs, core), (twin_refs, 1 - core)):
            for k, half_ref in zip(ORDER, half_refs):
                r = 2 * chip(place, k) + c
                half_scratch[s, :, pl.ds(pl.multiple_of(r * strip, strip), strip)] = half_ref[s]
        columns = pl.ds(pl.multiple_of(core * width, width), width)
        prec = jnp.dot(half_scratch[s], right_ref[s, :, columns], preferred_element_type=f32)
        back_ref[:, :, s * width : (s + 1) * width] = prec.reshape(owners, part, width).astype(bf16)
        prec_square = jnp.broadcast_to(jnp.sum(prec * prec, keepdims=True), (part, LANES))
        for k, term in enumerate(split3(square_ref[s]) + split3(prec_square)):
            tail = jnp.where(lane == TERMS * s + k, term, tail)
    back_ref[:, :, slots * width :] = jnp.broadcast_to(tail[None], (owners, part, LANES)).astype(bf16)


def select_kernel(slot, back_ref, tiles_ref, *, first):
    part, wide = back_ref.shape[1:]
    width = (wide - LANES) // 2
    each = width // LANES
    blocks = (tiles_ref.shape[0] - 1) // each
    lane = lax.broadcasted_iota(jnp.int32, (part, LANES), 1)
    line = lax.broadcasted_iota(jnp.int32, (part, LANES), 0)
    terms = jnp.zeros((part, LANES), f32)
    for b in range(blocks):
        q, h = slot[first + b], b % 2
        s = lax.rem(q, 2)
        for t in range(each):
            columns = pl.ds(pl.multiple_of(s * width + t * LANES, LANES), LANES)
            tiles_ref[b * each + t] = back_ref[q // 2, :, columns]
        tail = back_ref[q // 2, :, 2 * width :].astype(f32)
        tail = jnp.where(s == h, tail, pltpu.roll(tail, TERMS if h else LANES - TERMS, 1))
        here = (line == b // 2) & (lane >= TERMS * h) & (lane < TERMS * (h + 1))
        terms = jnp.where(here, tail, terms)
    tiles_ref[blocks * each] = terms.astype(bf16)


def finish_kernel(place, *refs, entries):
    out_ref, ready, ratios, written = refs[16:]
    part = refs[0].shape[1]
    mats, rows, full = ready.shape
    blocks = ratios.shape[0] // 2
    each = (refs[0].shape[0] - 1) // blocks
    some = mats // 2
    count = blocks // some
    lane = lax.broadcasted_iota(jnp.int32, (part, LANES), 1)

    def emit(m, row, own_refs, twin_refs, core, odd):
        couples = ((SELF, FAR), (OPPOSITE, NEAR)) if core else ((SELF, NEAR), (OPPOSITE, FAR))
        for couple in couples:
            at = pl.ds(pl.multiple_of(chip(place, couple[0]) // 2 * 2 * part, 2 * part), 2 * part)
            for j in range(count):
                b = m * count + j
                for found, c in ((own_refs, core), (twin_refs, 1 - core)):
                    for t in range(each):
                        tiles = [
                            found[k][b * each + t].astype(f32) * ratios[row * count + j]
                            for k in (couple[::-1] if odd else couple)
                        ]
                        columns = pl.ds(((2 * j + c) * each + t) * LANES, LANES)
                        ready[row, at, columns] = jnp.concatenate(tiles, 0).astype(bf16)

    def write(m):
        return pltpu.make_async_copy(ready.at[m], out_ref.at[m], written.at[m])

    for n in range(2):
        own_refs, twin_refs = refs[8 * n : 8 * n + 4], refs[8 * n + 4 : 8 * n + 8]
        tail = sum(ref[blocks * each].astype(f32) for ref in own_refs + twin_refs)
        for h in range(2):
            block_square, prec_square = [
                jnp.sum(jnp.where((lane >= start) & (lane < start + 3), tail, 0.0), axis=1, keepdims=True)
                for start in (TERMS * h, TERMS * h + 3)
            ]
            ratio = jnp.sqrt(block_square / entries + EPSILON) / jnp.sqrt(prec_square / entries + EPSILON)
            for line in range(part):
                ratios[blocks * n + 2 * line + h] = jnp.broadcast_to(ratio[line : line + 1], (part, LANES))

        @pl.loop(0, some)
        def _(m):
            for core in range(2):
                for odd in range(2):
                    here = (lax.rem(place[0], 2) == core) & (lax.rem(place[0] // 2, 2) == odd)
                    pl.when(here)(functools.partial(emit, m, some * n + m, own_refs, twin_refs, core, odd))
            write(some * n + m).start()

    for m in range(mats):
        write(m).wait()


def on_device(grads, left_root, right_root, block_slot):
    owners = lax.axis_size("fsdp")
    reps = lax.axis_size("replica")
    slots, height, width = left_root.shape[0], left_root.shape[1], right_root.shape[1]
    _, mats, rows, full = grads.shape
    cols = full // width
    blocks = mats * cols
    strip = width // reps
    part = rows // 4
    shape = jax.ShapeDtypeStruct

    place = lax.axis_index("replica").reshape(1).astype(jnp.int32)
    def twin(x):
        return lax.ppermute(x, "replica", [(i, i ^ 1) for i in range(reps)])

    def exchange(x, relative):
        perm = [(i, i ^ (2 * masks(i % 2)[relative])) for i in range(reps)]
        return lax.ppermute(x, "replica", perm)

    sizes = dict(cols=cols, width=width, strip=strip)
    def strips(*n):
        return shape((*n, mats, cols, rows, strip), bf16)

    def local(kernel, in_specs, out_specs, out_shape, scratch_shapes=()):
        return pl.pallas_call(
            kernel,
            in_specs=in_specs,
            out_specs=out_specs,
            out_shape=out_shape,
            scratch_shapes=scratch_shapes,
            compiler_params=pltpu.CompilerParams(vmem_limit_bytes=VMEM_BYTES),
        )

    smem, vmem = pl.BlockSpec(memory_space=pltpu.SMEM), pl.BlockSpec(memory_space=pltpu.VMEM)
    sums = {}
    for kinds in ((OPPOSITE, NEAR), (SELF, FAR)):
        send = local(
            functools.partial(send_kernel, kinds=kinds, **sizes),
            [smem, pl.BlockSpec(memory_space=pl.ANY)],
            vmem,
            strips(2),
            [pltpu.SemaphoreType.DMA((2 * cols,))],
        )(place, pltpu.with_memory_space_constraint(grads, pltpu.HBM))
        got = twin(send)
        found = local(
            functools.partial(pair_sum_kernel, kinds=kinds, **sizes), [smem, vmem, vmem], [vmem] * 2, [strips()] * 2
        )(place, grads, got)
        sums.update(zip(kinds, found))

    onward = exchange(sums[OPPOSITE], NEAR)
    direct = exchange(sums[NEAR], NEAR)
    passed = local(add_kernel, [vmem] * 2, vmem, strips())(sums[FAR], onward)
    last = exchange(passed, FAR)

    outgoing = local(route_kernel, [smem] + [vmem] * 3, vmem, shape((owners, slots, rows, strip), bf16))(
        block_slot, sums[SELF], direct, last
    )
    incoming = lax.all_to_all(outgoing, "fsdp", 0, 0, tiled=True)

    half_shape = shape((slots, owners * part, strip), bf16)
    *halves, square = local(
        left_kernel,
        [smem, vmem, vmem],
        [vmem] * 5,
        [half_shape] * 4 + [shape((slots, part, LANES), f32)],
        [pltpu.VMEM((slots, owners, 4, part, strip), f32)],
    )(place, left_root, incoming)
    halves = [half if k == SELF else exchange(half, k) for k, half in zip(ORDER, halves)]
    handed = [twin(halves[ORDER.index(k)]) for k in TWIN_ORDER]
    wide = width + LANES
    back = local(
        right_kernel,
        [smem] + [vmem] * 10,
        vmem,
        shape((owners, part, wide), bf16),
        [pltpu.VMEM((slots, owners * part, width), bf16)],
    )(place, *halves, *handed, right_root, square)
    back = lax.all_to_all(back, "fsdp", 0, 0, tiled=True)

    some = blocks // 2
    tiles = some * (width // 2 // LANES) + 1
    parts = [
        local(functools.partial(select_kernel, first=n * some), [smem, vmem], vmem, shape((tiles, part, LANES), bf16))(
            block_slot, back
        )
        for n in range(2)
    ]
    near = [exchange(x, NEAR) for x in parts]
    far = [exchange(lax.optimization_barrier((x, y))[0], FAR) for x, y in zip(parts, near)]
    opposite = [exchange(x, FAR) for x in near]
    pieces = []
    for n in range(2):
        pieces += [parts[n], near[n], far[n], opposite[n]]
        pieces += [twin(x) for x in (parts[n], far[n], near[n], opposite[n])]
    return local(
        functools.partial(finish_kernel, entries=height * width),
        [smem] + [vmem] * 16,
        pl.BlockSpec(memory_space=pl.ANY),
        shape((mats, rows, full), bf16),
        [
            pltpu.VMEM((mats, rows, full), bf16),
            pltpu.VMEM((blocks, part, LANES), f32),
            pltpu.SemaphoreType.DMA((mats,)),
        ],
    )(place, *pieces)


def solution(mesh):
    in_specs = (P("replica", None, "fsdp", None), P("fsdp", None, None), P("fsdp", None, None), P())
    return jax.shard_map(
        on_device, mesh=mesh, in_specs=in_specs, out_specs=P(None, "fsdp", None), check_vma=False
    )
```

```python
import functools
import jax
import jax.numpy as jnp
from jax import lax
from jax.experimental import pallas as pl
from jax.experimental.pallas import tpu as pltpu
from jax.sharding import PartitionSpec as P

EPSILON = 1e-06
LANES = 128
TERMS = 6
MIB = 1024 * 1024
VMEM_BYTES = 24 * MIB
bf16, f32 = jnp.bfloat16, jnp.float32

SELF, NEAR, FAR, OPPOSITE = range(4)
ORDER = (SELF, OPPOSITE, NEAR, FAR)
TWIN_ORDER = (SELF, OPPOSITE, FAR, NEAR)


CHIPS_X, CHIPS_Z, STEP_Z = 4, 8, 3


def place_of(owner):
    z, x = owner // CHIPS_X, owner % CHIPS_X
    return x * CHIPS_Z + STEP_Z * z % CHIPS_Z


def masks(core):
    return 0, 1 + 2 * core, 3 - 2 * core, 2


def chip(place, relative):
    return lax.bitwise_xor(place[0] // 2, jnp.int32(masks(lax.rem(place[0], 2))[relative]))


def strip_columns(place, relative, core, j, width, strip):
    index = 2 * chip(place, relative) + core
    return pl.ds(pl.multiple_of(j * width + index * strip, strip), strip)


def together(copies):
    copies = list(copies)
    for copy in copies:
        copy.start()
    for copy in copies:
        copy.wait()


def send_kernel(place, grads_ref, send_ref, arrived, *, kinds, cols, width, strip):
    other = 1 - lax.rem(place[0], 2)
    order = (SELF, FAR, NEAR, OPPOSITE)
    together(
        pltpu.make_async_copy(
            grads_ref.at[0, :, :, strip_columns(place, order[k], other, j, width, strip)],
            send_ref.at[n, :, j],
            arrived.at[n * cols + j],
        )
        for n, k in enumerate(kinds)
        for j in range(cols)
    )


def pair_sum_kernel(place, grads_ref, got_ref, *sum_refs, kinds, cols, width, strip):
    core = lax.rem(place[0], 2)
    for n, (k, sum_ref) in enumerate(zip(kinds, sum_refs)):
        for m in range(grads_ref.shape[1]):
            for j in range(cols):
                piece = grads_ref[0, m, :, strip_columns(place, k, core, j, width, strip)]
                sum_ref[m, j] = (piece.astype(f32) + got_ref[n, m, j].astype(f32)).astype(bf16)


def add_kernel(x_ref, y_ref, out_ref):
    out_ref[...] = (x_ref[...].astype(f32) + y_ref[...].astype(f32)).astype(bf16)


def route_kernel(slot, *refs):
    *terms, out_ref = refs
    slots = out_ref.shape[1]
    cols = terms[0].shape[1]
    out_ref[...] = jnp.zeros_like(out_ref)
    for m in range(terms[0].shape[0]):
        for j in range(cols):
            q = slot[m * cols + j]
            total = sum(term[m, j].astype(f32) for term in terms)
            out_ref[place_of(q // slots), lax.rem(q, slots)] = total.astype(bf16)


def left_kernel(place, left_ref, block_ref, *out_refs):
    *half_refs, square_ref, scratch = out_refs
    owners, slots, rows, strip = block_ref.shape
    for s in range(slots):
        block = jnp.concatenate([block_ref[place_of(owner), s] for owner in range(owners)], axis=0)
        wide = block.astype(f32)
        square_ref[s] = jnp.broadcast_to(jnp.sum(wide * wide, keepdims=True), square_ref.shape[1:])
        half = jnp.dot(left_ref[s], block, preferred_element_type=f32)
        scratch[s] = half.reshape(scratch.shape[1:])
        for k, half_ref in zip(ORDER, half_refs):
            half_ref[s] = scratch[s, :, chip(place, k)].reshape(half_ref.shape[1:]).astype(bf16)


def split3(x):
    a = x.astype(bf16).astype(f32)
    b = (x - a).astype(bf16).astype(f32)
    return a, b, x - a - b


def right_kernel(place, *refs):
    own_refs, twin_refs = refs[:4], refs[4:8]
    right_ref, square_ref, back_ref, half_scratch = refs[8:]
    owners, part, wide = back_ref.shape
    slots = right_ref.shape[0]
    width = (wide - LANES) // slots
    strip = own_refs[0].shape[2]
    core = lax.rem(place[0], 2)
    lane = lax.broadcasted_iota(jnp.int32, (part, LANES), 1)
    tail = jnp.zeros((part, LANES), f32)
    for s in range(slots):
        for half_refs, c in ((own_refs, core), (twin_refs, 1 - core)):
            for k, half_ref in zip(ORDER, half_refs):
                r = 2 * chip(place, k) + c
                half_scratch[s, :, pl.ds(pl.multiple_of(r * strip, strip), strip)] = half_ref[s]
        columns = pl.ds(pl.multiple_of(core * width, width), width)
        prec = jnp.dot(half_scratch[s], right_ref[s, :, columns], preferred_element_type=f32)
        rows = prec.reshape(owners, part, width).astype(bf16)
        for owner in range(owners):
            back_ref[place_of(owner), :, s * width : (s + 1) * width] = rows[owner]
        prec_square = jnp.broadcast_to(jnp.sum(prec * prec, keepdims=True), (part, LANES))
        for k, term in enumerate(split3(square_ref[s]) + split3(prec_square)):
            tail = jnp.where(lane == TERMS * s + k, term, tail)
    back_ref[:, :, slots * width :] = jnp.broadcast_to(tail[None], (owners, part, LANES)).astype(bf16)


def select_kernel(slot, back_ref, tiles_ref):
    part, wide = back_ref.shape[1:]
    width = (wide - LANES) // 2
    each = width // LANES
    blocks = (tiles_ref.shape[0] - 2) // each
    lane = lax.broadcasted_iota(jnp.int32, (part, LANES), 1)
    line = lax.broadcasted_iota(jnp.int32, (part, LANES), 0)
    terms = [jnp.zeros((part, LANES), f32)] * 2
    for b in range(blocks):
        q, h, pair = slot[b], b % 2, b // 2
        s = lax.rem(q, 2)
        for t in range(each):
            columns = pl.ds(pl.multiple_of(s * width + t * LANES, LANES), LANES)
            tiles_ref[b * each + t] = back_ref[place_of(q // 2), :, columns]
        tail = back_ref[place_of(q // 2), :, 2 * width :].astype(f32)
        tail = jnp.where(s == h, tail, pltpu.roll(tail, TERMS if h else LANES - TERMS, 1))
        here = (line == pair % part) & (lane >= TERMS * h) & (lane < TERMS * (h + 1))
        terms[pair // part] = jnp.where(here, tail, terms[pair // part])
    for n in range(2):
        tiles_ref[blocks * each + n] = terms[n].astype(bf16)


def finish_kernel(place, *refs, entries):
    own_refs, twin_refs = refs[:4], refs[4:8]
    out_ref, ready, ratios, written = refs[8:]
    part = own_refs[0].shape[1]
    mats, rows, full = ready.shape
    blocks = ratios.shape[0]
    each = (own_refs[0].shape[0] - 2) // blocks
    count = blocks // mats
    lane = lax.broadcasted_iota(jnp.int32, (part, LANES), 1)
    for n in range(2):
        tail = sum(ref[blocks * each + n].astype(f32) for ref in own_refs + twin_refs)
        for h in range(2):
            block_square, prec_square = [
                jnp.sum(jnp.where((lane >= start) & (lane < start + 3), tail, 0.0), axis=1, keepdims=True)
                for start in (TERMS * h, TERMS * h + 3)
            ]
            ratio = jnp.sqrt(block_square / entries + EPSILON) / jnp.sqrt(prec_square / entries + EPSILON)
            for line in range(part):
                ratios[2 * (n * part + line) + h] = jnp.broadcast_to(ratio[line : line + 1], (part, LANES))

    def emit(m, core, odd):
        couples = ((SELF, FAR), (OPPOSITE, NEAR)) if core else ((SELF, NEAR), (OPPOSITE, FAR))
        for couple in couples:
            at = pl.ds(pl.multiple_of(chip(place, couple[0]) // 2 * 2 * part, 2 * part), 2 * part)
            for j in range(count):
                b = m * count + j
                for refs, c in ((own_refs, core), (twin_refs, 1 - core)):
                    for t in range(each):
                        tiles = [
                            refs[k][b * each + t].astype(f32) * ratios[b] for k in (couple[::-1] if odd else couple)
                        ]
                        columns = pl.ds(((2 * j + c) * each + t) * LANES, LANES)
                        ready[m, at, columns] = jnp.concatenate(tiles, 0).astype(bf16)

    def write(m):
        return pltpu.make_async_copy(ready.at[m], out_ref.at[m], written.at[m])

    @pl.loop(0, mats)
    def _(m):
        for core in range(2):
            for odd in range(2):
                here = (lax.rem(place[0], 2) == core) & (lax.rem(place[0] // 2, 2) == odd)
                pl.when(here)(functools.partial(emit, m, core, odd))
        write(m).start()

    for m in range(mats):
        write(m).wait()


def on_device(grads, left_root, right_root, block_slot):
    owners = lax.axis_size("fsdp")
    reps = lax.axis_size("replica")
    slots, height, width = left_root.shape[0], left_root.shape[1], right_root.shape[1]
    _, mats, rows, full = grads.shape
    cols = full // width
    blocks = mats * cols
    strip = width // reps
    part = rows // 4
    shape = jax.ShapeDtypeStruct

    place = lax.axis_index("replica").reshape(1).astype(jnp.int32)
    def twin(x):
        return lax.ppermute(x, "replica", [(i, i ^ 1) for i in range(reps)])

    def exchange(x, relative):
        perm = [(i, i ^ (2 * masks(i % 2)[relative])) for i in range(reps)]
        return lax.ppermute(x, "replica", perm)

    sizes = dict(cols=cols, width=width, strip=strip)
    def strips(*n):
        return shape((*n, mats, cols, rows, strip), bf16)

    def local(kernel, in_specs, out_specs, out_shape, scratch_shapes=()):
        return pl.pallas_call(
            kernel,
            in_specs=in_specs,
            out_specs=out_specs,
            out_shape=out_shape,
            scratch_shapes=scratch_shapes,
            compiler_params=pltpu.CompilerParams(vmem_limit_bytes=VMEM_BYTES),
        )

    smem, vmem = pl.BlockSpec(memory_space=pltpu.SMEM), pl.BlockSpec(memory_space=pltpu.VMEM)
    sums = {}
    for kinds in ((OPPOSITE, NEAR), (SELF, FAR)):
        send = local(
            functools.partial(send_kernel, kinds=kinds, **sizes),
            [smem, pl.BlockSpec(memory_space=pl.ANY)],
            vmem,
            strips(2),
            [pltpu.SemaphoreType.DMA((2 * cols,))],
        )(place, pltpu.with_memory_space_constraint(grads, pltpu.HBM))
        got = twin(send)
        found = local(
            functools.partial(pair_sum_kernel, kinds=kinds, **sizes), [smem, vmem, vmem], [vmem] * 2, [strips()] * 2
        )(place, grads, got)
        sums.update(zip(kinds, found))

    onward = exchange(sums[OPPOSITE], NEAR)
    direct = exchange(sums[NEAR], NEAR)
    passed = local(add_kernel, [vmem] * 2, vmem, strips())(sums[FAR], onward)
    last = exchange(passed, FAR)

    outgoing = local(route_kernel, [smem] + [vmem] * 3, vmem, shape((owners, slots, rows, strip), bf16))(
        block_slot, sums[SELF], direct, last
    )
    ring = [sorted(range(owners), key=place_of)]
    incoming = lax.all_to_all(outgoing, "fsdp", 0, 0, tiled=True, axis_index_groups=ring)

    half_shape = shape((slots, owners * part, strip), bf16)
    *halves, square = local(
        left_kernel,
        [smem, vmem, vmem],
        [vmem] * 5,
        [half_shape] * 4 + [shape((slots, part, LANES), f32)],
        [pltpu.VMEM((slots, owners, 4, part, strip), f32)],
    )(place, left_root, incoming)
    halves = [half if k == SELF else exchange(half, k) for k, half in zip(ORDER, halves)]
    handed = [twin(halves[ORDER.index(k)]) for k in TWIN_ORDER]
    wide = width + LANES
    back = local(
        right_kernel,
        [smem] + [vmem] * 10,
        vmem,
        shape((owners, part, wide), bf16),
        [pltpu.VMEM((slots, owners * part, width), bf16)],
    )(place, *halves, *handed, right_root, square)
    back = lax.all_to_all(back, "fsdp", 0, 0, tiled=True, axis_index_groups=ring)

    tiles = blocks * (width // 2 // LANES) + 2
    mine = local(select_kernel, [smem, vmem], vmem, shape((tiles, part, LANES), bf16))(block_slot, back)
    near = exchange(mine, NEAR)
    far = exchange(mine, FAR)
    opposite = exchange(near, FAR)
    own = [mine, near, far, opposite]
    other = [twin(x) for x in (mine, far, near, opposite)]
    return local(
        functools.partial(finish_kernel, entries=height * width),
        [smem] + [vmem] * 8,
        pl.BlockSpec(memory_space=pl.ANY),
        shape((mats, rows, full), bf16),
        [
            pltpu.VMEM((mats, rows, full), bf16),
            pltpu.VMEM((blocks, part, LANES), f32),
            pltpu.SemaphoreType.DMA((mats,)),
        ],
    )(place, *own, *other)


def solution(mesh):
    in_specs = (P("replica", None, "fsdp", None), P("fsdp", None, None), P("fsdp", None, None), P())
    return jax.shard_map(
        on_device, mesh=mesh, in_specs=in_specs, out_specs=P(None, "fsdp", None), check_vma=False
    )
```

```python
import functools
import jax
import jax.numpy as jnp
from jax import lax
from jax.experimental import pallas as pl
from jax.experimental.pallas import tpu as pltpu
from jax.sharding import PartitionSpec as P

EPSILON = 1e-06
LANES = 128
TERMS = 6
MIB = 1024 * 1024
VMEM_BYTES = 24 * MIB
bf16, f32 = jnp.bfloat16, jnp.float32

SELF, NEAR, FAR, OPPOSITE = range(4)
ORDER = (SELF, OPPOSITE, NEAR, FAR)
TWIN_ORDER = (SELF, OPPOSITE, FAR, NEAR)


def masks(core):
    return 0, 1 + 2 * core, 3 - 2 * core, 2


def chip(place, relative):
    return lax.bitwise_xor(place[0] // 2, jnp.int32(masks(lax.rem(place[0], 2))[relative]))


def strip_index(place, relative, core):
    return 2 * chip(place, relative) + core


def together(copies):
    copies = list(copies)
    for copy in copies:
        copy.start()
    for copy in copies:
        copy.wait()


def send_kernel(place, grads_ref, send_ref, arrived, *, kinds):
    other = 1 - lax.rem(place[0], 2)
    order = (SELF, FAR, NEAR, OPPOSITE)
    together(
        pltpu.make_async_copy(
            grads_ref.at[:, :, :, strip_index(place, order[k], other)], send_ref.at[n], arrived.at[n]
        )
        for n, k in enumerate(kinds)
    )


def pair_sum_kernel(place, grads_ref, got_ref, *sum_refs, kinds):
    core = lax.rem(place[0], 2)
    for n, (k, sum_ref) in enumerate(zip(kinds, sum_refs)):
        piece = grads_ref[:, :, :, strip_index(place, k, core)]
        sum_ref[...] = (piece.astype(f32) + got_ref[n].astype(f32)).astype(bf16)


def add_kernel(x_ref, y_ref, out_ref):
    out_ref[...] = (x_ref[...].astype(f32) + y_ref[...].astype(f32)).astype(bf16)


def route_kernel(slot, *refs):
    *terms, out_ref = refs
    slots = out_ref.shape[1]
    cols = terms[0].shape[2]
    out_ref[...] = jnp.zeros_like(out_ref)
    for m in range(terms[0].shape[0]):
        for j in range(cols):
            q = slot[m * cols + j]
            total = sum(term[m, :, j].astype(f32) for term in terms)
            out_ref[q // slots, lax.rem(q, slots)] = total.reshape(out_ref.shape[2:]).astype(bf16)


def left_kernel(place, left_ref, block_ref, *out_refs):
    *half_refs, square_ref, scratch = out_refs
    owners, slots, rows, strip = block_ref.shape
    for s in range(slots):
        block = block_ref[:, s].reshape(owners * rows, strip)
        wide = block.astype(f32)
        square_ref[s] = jnp.broadcast_to(jnp.sum(wide * wide, keepdims=True), square_ref.shape[1:])
        half = jnp.dot(left_ref[s], block, preferred_element_type=f32)
        scratch[s] = half.reshape(scratch.shape[1:])
        for k, half_ref in zip(ORDER, half_refs):
            half_ref[s] = scratch[s, :, chip(place, k)].reshape(half_ref.shape[1:]).astype(bf16)


def split3(x):
    a = x.astype(bf16).astype(f32)
    b = (x - a).astype(bf16).astype(f32)
    return a, b, x - a - b


def right_kernel(place, *refs):
    own_refs, twin_refs = refs[:4], refs[4:8]
    right_ref, square_ref, back_ref, half_scratch = refs[8:]
    owners, part, wide = back_ref.shape
    slots = right_ref.shape[0]
    width = (wide - LANES) // slots
    strip = own_refs[0].shape[2]
    core = lax.rem(place[0], 2)
    lane = lax.broadcasted_iota(jnp.int32, (part, LANES), 1)
    tail = jnp.zeros((part, LANES), f32)
    for s in range(slots):
        for half_refs, c in ((own_refs, core), (twin_refs, 1 - core)):
            for k, half_ref in zip(ORDER, half_refs):
                r = 2 * chip(place, k) + c
                half_scratch[s, :, pl.ds(pl.multiple_of(r * strip, strip), strip)] = half_ref[s]
        columns = pl.ds(pl.multiple_of(core * width, width), width)
        prec = jnp.dot(half_scratch[s], right_ref[s, :, columns], preferred_element_type=f32)
        back_ref[:, :, s * width : (s + 1) * width] = prec.reshape(owners, part, width).astype(bf16)
        prec_square = jnp.broadcast_to(jnp.sum(prec * prec, keepdims=True), (part, LANES))
        for k, term in enumerate(split3(square_ref[s]) + split3(prec_square)):
            tail = jnp.where(lane == TERMS * s + k, term, tail)
    back_ref[:, :, slots * width :] = jnp.broadcast_to(tail[None], (owners, part, LANES)).astype(bf16)


def select_kernel(slot, back_ref, tiles_ref):
    part, wide = back_ref.shape[1:]
    width = (wide - LANES) // 2
    each = width // LANES
    blocks = (tiles_ref.shape[0] - 2) // each
    lane = lax.broadcasted_iota(jnp.int32, (part, LANES), 1)
    line = lax.broadcasted_iota(jnp.int32, (part, LANES), 0)
    terms = [jnp.zeros((part, LANES), f32)] * 2
    for b in range(blocks):
        q, h, pair = slot[b], b % 2, b // 2
        s = lax.rem(q, 2)
        for t in range(each):
            columns = pl.ds(pl.multiple_of(s * width + t * LANES, LANES), LANES)
            tiles_ref[b * each + t] = back_ref[q // 2, :, columns]
        tail = back_ref[q // 2, :, 2 * width :].astype(f32)
        tail = jnp.where(s == h, tail, pltpu.roll(tail, TERMS if h else LANES - TERMS, 1))
        here = (line == pair % part) & (lane >= TERMS * h) & (lane < TERMS * (h + 1))
        terms[pair // part] = jnp.where(here, tail, terms[pair // part])
    for n in range(2):
        tiles_ref[blocks * each + n] = terms[n].astype(bf16)


def finish_kernel(place, *refs, entries):
    own_refs, twin_refs = refs[:4], refs[4:8]
    out_ref, ready, ratios, written = refs[8:]
    part = own_refs[0].shape[1]
    mats, rows, full = ready.shape
    blocks = ratios.shape[0]
    each = (own_refs[0].shape[0] - 2) // blocks
    count = blocks // mats
    lane = lax.broadcasted_iota(jnp.int32, (part, LANES), 1)
    for n in range(2):
        tail = sum(ref[blocks * each + n].astype(f32) for ref in own_refs + twin_refs)
        for h in range(2):
            block_square, prec_square = [
                jnp.sum(jnp.where((lane >= start) & (lane < start + 3), tail, 0.0), axis=1, keepdims=True)
                for start in (TERMS * h, TERMS * h + 3)
            ]
            ratio = jnp.sqrt(block_square / entries + EPSILON) / jnp.sqrt(prec_square / entries + EPSILON)
            for line in range(part):
                ratios[2 * (n * part + line) + h] = jnp.broadcast_to(ratio[line : line + 1], (part, LANES))

    def emit(m, core, odd):
        couples = ((SELF, FAR), (OPPOSITE, NEAR)) if core else ((SELF, NEAR), (OPPOSITE, FAR))
        for couple in couples:
            side = chip(place, couple[0]) // 2
            at = lines(side)
            for j in range(count):
                b = m * count + j
                for refs, c in ((own_refs, core), (twin_refs, 1 - core)):
                    for t in range(each):
                        tiles = [
                            refs[k][b * each + t].astype(f32) * ratios[b] for k in (couple[::-1] if odd else couple)
                        ]
                        columns = pl.ds(((2 * j + c) * each + t) * LANES, LANES)
                        ready[m, at, columns] = jnp.concatenate(tiles, 0).astype(bf16)
            write(m, side).start()

    def lines(side):
        return pl.ds(pl.multiple_of(side * 2 * part, 2 * part), 2 * part)

    def write(m, side):
        return pltpu.make_async_copy(ready.at[m, lines(side)], out_ref.at[m, lines(side)], written.at[m, side])

    @pl.loop(0, mats)
    def _(m):
        for core in range(2):
            for odd in range(2):
                here = (lax.rem(place[0], 2) == core) & (lax.rem(place[0] // 2, 2) == odd)
                pl.when(here)(functools.partial(emit, m, core, odd))

    for m in range(mats):
        for side in range(2):
            write(m, side).wait()


def on_device(grads, left_root, right_root, block_slot):
    owners = lax.axis_size("fsdp")
    reps = lax.axis_size("replica")
    slots, height, width = left_root.shape[0], left_root.shape[1], right_root.shape[1]
    _, mats, rows, full = grads.shape
    cols = full // width
    blocks = mats * cols
    strip = width // reps
    part = rows // 4
    shape = jax.ShapeDtypeStruct

    place = lax.axis_index("replica").reshape(1).astype(jnp.int32)
    def twin(x):
        return lax.ppermute(x, "replica", [(i, i ^ 1) for i in range(reps)])

    def exchange(x, relative):
        perm = [(i, i ^ (2 * masks(i % 2)[relative])) for i in range(reps)]
        return lax.ppermute(x, "replica", perm)

    group = 8
    tiles = grads.reshape(mats, rows // group, group, cols, reps, strip).transpose(0, 1, 3, 4, 2, 5)

    def strips(*n):
        return shape((*n, mats, rows // group, cols, group, strip), bf16)

    def local(kernel, in_specs, out_specs, out_shape, scratch_shapes=()):
        return pl.pallas_call(
            kernel,
            in_specs=in_specs,
            out_specs=out_specs,
            out_shape=out_shape,
            scratch_shapes=scratch_shapes,
            compiler_params=pltpu.CompilerParams(vmem_limit_bytes=VMEM_BYTES),
        )

    smem, vmem = pl.BlockSpec(memory_space=pltpu.SMEM), pl.BlockSpec(memory_space=pltpu.VMEM)
    sums = {}
    for kinds in ((OPPOSITE, NEAR), (SELF, FAR)):
        send = local(
            functools.partial(send_kernel, kinds=kinds),
            [smem, pl.BlockSpec(memory_space=pl.ANY)],
            vmem,
            strips(2),
            [pltpu.SemaphoreType.DMA((2,))],
        )(place, pltpu.with_memory_space_constraint(tiles, pltpu.HBM))
        got = twin(send)
        found = local(
            functools.partial(pair_sum_kernel, kinds=kinds), [smem, vmem, vmem], [vmem] * 2, [strips()] * 2
        )(place, tiles, got)
        sums.update(zip(kinds, found))

    onward = exchange(sums[OPPOSITE], NEAR)
    direct = exchange(sums[NEAR], NEAR)
    passed = local(add_kernel, [vmem] * 2, vmem, strips())(sums[FAR], onward)
    last = exchange(passed, FAR)

    outgoing = local(route_kernel, [smem] + [vmem] * 3, vmem, shape((owners, slots, rows, strip), bf16))(
        block_slot, sums[SELF], direct, last
    )
    incoming = lax.all_to_all(outgoing, "fsdp", 0, 0, tiled=True)

    half_shape = shape((slots, owners * part, strip), bf16)
    *halves, square = local(
        left_kernel,
        [smem, vmem, vmem],
        [vmem] * 5,
        [half_shape] * 4 + [shape((slots, part, LANES), f32)],
        [pltpu.VMEM((slots, owners, 4, part, strip), f32)],
    )(place, left_root, incoming)
    halves = [half if k == SELF else exchange(half, k) for k, half in zip(ORDER, halves)]
    handed = [twin(halves[ORDER.index(k)]) for k in TWIN_ORDER]
    wide = width + LANES
    back = local(
        right_kernel,
        [smem] + [vmem] * 10,
        vmem,
        shape((owners, part, wide), bf16),
        [pltpu.VMEM((slots, owners * part, width), bf16)],
    )(place, *halves, *handed, right_root, square)
    back = lax.all_to_all(back, "fsdp", 0, 0, tiled=True)

    tiles = blocks * (width // 2 // LANES) + 2
    mine = local(select_kernel, [smem, vmem], vmem, shape((tiles, part, LANES), bf16))(block_slot, back)
    near = exchange(mine, NEAR)
    far = exchange(mine, FAR)
    opposite = exchange(near, FAR)
    own = [mine, near, far, opposite]
    other = [twin(x) for x in (mine, far, near, opposite)]
    return local(
        functools.partial(finish_kernel, entries=height * width),
        [smem] + [vmem] * 8,
        pl.BlockSpec(memory_space=pl.ANY),
        shape((mats, rows, full), bf16),
        [
            pltpu.VMEM((mats, rows, full), bf16),
            pltpu.VMEM((blocks, part, LANES), f32),
            pltpu.SemaphoreType.DMA((mats, 2)),
        ],
    )(place, *own, *other)


def solution(mesh):
    in_specs = (P("replica", None, "fsdp", None), P("fsdp", None, None), P("fsdp", None, None), P())
    return jax.shard_map(
        on_device, mesh=mesh, in_specs=in_specs, out_specs=P(None, "fsdp", None), check_vma=False
    )
```

```python
import functools
import jax
import jax.numpy as jnp
from jax import lax
from jax.experimental import pallas as pl
from jax.experimental.pallas import tpu as pltpu
from jax.sharding import PartitionSpec as P

EPSILON = 1e-06
LANES = 128
TERMS = 6
MIB = 1024 * 1024
VMEM_BYTES = 24 * MIB
bf16, f32 = jnp.bfloat16, jnp.float32

SELF, NEAR, FAR, OPPOSITE = range(4)
ORDER = (SELF, OPPOSITE, NEAR, FAR)
TWIN_ORDER = (SELF, OPPOSITE, FAR, NEAR)
LAST = NEAR


def masks(core):
    return 0, 1 + 2 * core, 3 - 2 * core, 2


def chip(place, relative):
    return lax.bitwise_xor(place[0] // 2, jnp.int32(masks(lax.rem(place[0], 2))[relative]))


def strip_index(place, relative, core):
    return 2 * chip(place, relative) + core


def together(copies):
    copies = list(copies)
    for copy in copies:
        copy.start()
    for copy in copies:
        copy.wait()


def send_kernel(place, grads_ref, send_ref, arrived, *, kinds):
    other = 1 - lax.rem(place[0], 2)
    order = (SELF, FAR, NEAR, OPPOSITE)
    together(
        pltpu.make_async_copy(
            grads_ref.at[:, :, :, strip_index(place, order[k], other)], send_ref.at[n], arrived.at[n]
        )
        for n, k in enumerate(kinds)
    )


def pair_sum_kernel(place, grads_ref, got_ref, *sum_refs, kinds):
    core = lax.rem(place[0], 2)
    for n, (k, sum_ref) in enumerate(zip(kinds, sum_refs)):
        piece = grads_ref[:, :, :, strip_index(place, k, core)]
        sum_ref[...] = (piece.astype(f32) + got_ref[n].astype(f32)).astype(bf16)


def add_kernel(x_ref, y_ref, out_ref):
    out_ref[...] = (x_ref[...].astype(f32) + y_ref[...].astype(f32)).astype(bf16)


def route_kernel(slot, *refs):
    *terms, out_ref = refs
    slots = out_ref.shape[1]
    cols = terms[0].shape[2]
    out_ref[...] = jnp.zeros_like(out_ref)
    for m in range(terms[0].shape[0]):
        for j in range(cols):
            q = slot[m * cols + j]
            total = sum(term[m, :, j].astype(f32) for term in terms)
            out_ref[q // slots, lax.rem(q, slots)] = total.reshape(out_ref.shape[2:]).astype(bf16)


def left_kernel(place, left_ref, block_ref, *out_refs):
    *half_refs, square_ref, scratch = out_refs
    owners, slots, rows, strip = block_ref.shape
    for s in range(slots):
        block = block_ref[:, s].reshape(owners * rows, strip)
        wide = block.astype(f32)
        square_ref[s] = jnp.broadcast_to(jnp.sum(wide * wide, keepdims=True), square_ref.shape[1:])
        half = jnp.dot(left_ref[s], block, preferred_element_type=f32)
        scratch[s] = half.reshape(scratch.shape[1:])
        for k, half_ref in zip(ORDER, half_refs):
            half_ref[s] = scratch[s, :, chip(place, k)].reshape(half_ref.shape[1:]).astype(bf16)


def split3(x):
    a = x.astype(bf16).astype(f32)
    b = (x - a).astype(bf16).astype(f32)
    return a, b, x - a - b


def right_columns(place, right_ref):
    width = right_ref.shape[2] // 2
    return pl.ds(pl.multiple_of(lax.rem(place[0], 2) * width, width), width)


def strip_lines(place, relative, core, strip):
    return pl.ds(pl.multiple_of(strip_index(place, relative, core) * strip, strip), strip)


def right_kernel(place, *refs):
    *half_refs, right_ref, prec_ref, half_scratch = refs
    slots, _, strip = half_refs[0].shape
    core = lax.rem(place[0], 2)
    known = [(core, k) for k in ORDER] + [(1 - core, k) for k in ORDER if k != LAST]
    for s in range(slots):
        half_scratch[s, :, strip_lines(place, LAST, 1 - core, strip)] = jnp.zeros(half_refs[0].shape[1:], bf16)
        for half_ref, (c, k) in zip(half_refs, known):
            half_scratch[s, :, strip_lines(place, k, c, strip)] = half_ref[s]
        prec_ref[s] = jnp.dot(
            half_scratch[s], right_ref[s, :, right_columns(place, right_ref)], preferred_element_type=f32
        )


def last_strip_kernel(place, half_ref, right_ref, prec_ref, square_ref, back_ref):
    owners, part, wide = back_ref.shape
    slots, _, strip = half_ref.shape
    width = (wide - LANES) // slots
    lane = lax.broadcasted_iota(jnp.int32, (part, LANES), 1)
    tail = jnp.zeros((part, LANES), f32)
    lines = strip_lines(place, LAST, 1 - lax.rem(place[0], 2), strip)
    for s in range(slots):
        root = right_ref[s, lines, right_columns(place, right_ref)]
        prec = prec_ref[s] + jnp.dot(half_ref[s], root, preferred_element_type=f32)
        back_ref[:, :, s * width : (s + 1) * width] = prec.reshape(owners, part, width).astype(bf16)
        prec_square = jnp.broadcast_to(jnp.sum(prec * prec, keepdims=True), (part, LANES))
        for k, term in enumerate(split3(square_ref[s]) + split3(prec_square)):
            tail = jnp.where(lane == TERMS * s + k, term, tail)
    back_ref[:, :, slots * width :] = jnp.broadcast_to(tail[None], (owners, part, LANES)).astype(bf16)


def select_kernel(slot, back_ref, tiles_ref):
    part, wide = back_ref.shape[1:]
    width = (wide - LANES) // 2
    each = width // LANES
    blocks = (tiles_ref.shape[0] - 2) // each
    lane = lax.broadcasted_iota(jnp.int32, (part, LANES), 1)
    line = lax.broadcasted_iota(jnp.int32, (part, LANES), 0)
    terms = [jnp.zeros((part, LANES), f32)] * 2
    for b in range(blocks):
        q, h, pair = slot[b], b % 2, b // 2
        s = lax.rem(q, 2)
        for t in range(each):
            columns = pl.ds(pl.multiple_of(s * width + t * LANES, LANES), LANES)
            tiles_ref[b * each + t] = back_ref[q // 2, :, columns]
        tail = back_ref[q // 2, :, 2 * width :].astype(f32)
        tail = jnp.where(s == h, tail, pltpu.roll(tail, TERMS if h else LANES - TERMS, 1))
        here = (line == pair % part) & (lane >= TERMS * h) & (lane < TERMS * (h + 1))
        terms[pair // part] = jnp.where(here, tail, terms[pair // part])
    for n in range(2):
        tiles_ref[blocks * each + n] = terms[n].astype(bf16)


def finish_kernel(place, *refs, entries):
    own_refs, twin_refs = refs[:4], refs[4:8]
    out_ref, ready, ratios, written = refs[8:]
    part = own_refs[0].shape[1]
    mats, rows, full = ready.shape
    blocks = ratios.shape[0]
    each = (own_refs[0].shape[0] - 2) // blocks
    count = blocks // mats
    lane = lax.broadcasted_iota(jnp.int32, (part, LANES), 1)
    for n in range(2):
        tail = sum(ref[blocks * each + n].astype(f32) for ref in own_refs + twin_refs)
        for h in range(2):
            block_square, prec_square = [
                jnp.sum(jnp.where((lane >= start) & (lane < start + 3), tail, 0.0), axis=1, keepdims=True)
                for start in (TERMS * h, TERMS * h + 3)
            ]
            ratio = jnp.sqrt(block_square / entries + EPSILON) / jnp.sqrt(prec_square / entries + EPSILON)
            for line in range(part):
                ratios[2 * (n * part + line) + h] = jnp.broadcast_to(ratio[line : line + 1], (part, LANES))

    def emit(m, core, odd):
        couples = ((SELF, FAR), (OPPOSITE, NEAR)) if core else ((SELF, NEAR), (OPPOSITE, FAR))
        for couple in couples:
            side = chip(place, couple[0]) // 2
            at = lines(side)
            for j in range(count):
                b = m * count + j
                for refs, c in ((own_refs, core), (twin_refs, 1 - core)):
                    for t in range(each):
                        tiles = [
                            refs[k][b * each + t].astype(f32) * ratios[b] for k in (couple[::-1] if odd else couple)
                        ]
                        columns = pl.ds(((2 * j + c) * each + t) * LANES, LANES)
                        ready[m, at, columns] = jnp.concatenate(tiles, 0).astype(bf16)
            write(m, side).start()

    def lines(side):
        return pl.ds(pl.multiple_of(side * 2 * part, 2 * part), 2 * part)

    def write(m, side):
        return pltpu.make_async_copy(ready.at[m, lines(side)], out_ref.at[m, lines(side)], written.at[m, side])

    @pl.loop(0, mats)
    def _(m):
        for core in range(2):
            for odd in range(2):
                here = (lax.rem(place[0], 2) == core) & (lax.rem(place[0] // 2, 2) == odd)
                pl.when(here)(functools.partial(emit, m, core, odd))

    for m in range(mats):
        for side in range(2):
            write(m, side).wait()


def on_device(grads, left_root, right_root, block_slot):
    owners = lax.axis_size("fsdp")
    reps = lax.axis_size("replica")
    slots, height, width = left_root.shape[0], left_root.shape[1], right_root.shape[1]
    _, mats, rows, full = grads.shape
    cols = full // width
    blocks = mats * cols
    strip = width // reps
    part = rows // 4
    shape = jax.ShapeDtypeStruct

    place = lax.axis_index("replica").reshape(1).astype(jnp.int32)
    def twin(x):
        return lax.ppermute(x, "replica", [(i, i ^ 1) for i in range(reps)])

    def exchange(x, relative):
        perm = [(i, i ^ (2 * masks(i % 2)[relative])) for i in range(reps)]
        return lax.ppermute(x, "replica", perm)

    group = 8
    tiles = grads.reshape(mats, rows // group, group, cols, reps, strip).transpose(0, 1, 3, 4, 2, 5)

    def strips(*n):
        return shape((*n, mats, rows // group, cols, group, strip), bf16)

    def local(kernel, in_specs, out_specs, out_shape, scratch_shapes=()):
        return pl.pallas_call(
            kernel,
            in_specs=in_specs,
            out_specs=out_specs,
            out_shape=out_shape,
            scratch_shapes=scratch_shapes,
            compiler_params=pltpu.CompilerParams(vmem_limit_bytes=VMEM_BYTES),
        )

    smem, vmem = pl.BlockSpec(memory_space=pltpu.SMEM), pl.BlockSpec(memory_space=pltpu.VMEM)
    sums = {}
    for kinds in ((OPPOSITE, NEAR), (SELF, FAR)):
        send = local(
            functools.partial(send_kernel, kinds=kinds),
            [smem, pl.BlockSpec(memory_space=pl.ANY)],
            vmem,
            strips(2),
            [pltpu.SemaphoreType.DMA((2,))],
        )(place, pltpu.with_memory_space_constraint(tiles, pltpu.HBM))
        got = twin(send)
        found = local(
            functools.partial(pair_sum_kernel, kinds=kinds), [smem, vmem, vmem], [vmem] * 2, [strips()] * 2
        )(place, tiles, got)
        sums.update(zip(kinds, found))

    onward = exchange(sums[OPPOSITE], NEAR)
    direct = exchange(sums[NEAR], NEAR)
    passed = local(add_kernel, [vmem] * 2, vmem, strips())(sums[FAR], onward)
    last = exchange(passed, FAR)

    outgoing = local(route_kernel, [smem] + [vmem] * 3, vmem, shape((owners, slots, rows, strip), bf16))(
        block_slot, sums[SELF], direct, last
    )
    incoming = lax.all_to_all(outgoing, "fsdp", 0, 0, tiled=True)

    half_shape = shape((slots, owners * part, strip), bf16)
    *halves, square = local(
        left_kernel,
        [smem, vmem, vmem],
        [vmem] * 5,
        [half_shape] * 4 + [shape((slots, part, LANES), f32)],
        [pltpu.VMEM((slots, owners, 4, part, strip), f32)],
    )(place, left_root, incoming)
    halves = [half if k == SELF else exchange(half, k) for k, half in zip(ORDER, halves)]
    handed = [twin(halves[ORDER.index(k)]) for k in TWIN_ORDER]
    wide = width + LANES
    last = handed.pop(ORDER.index(LAST))
    prec = local(
        right_kernel,
        [smem] + [vmem] * 8,
        vmem,
        shape((slots, owners * part, width // 2), f32),
        [pltpu.VMEM((slots, owners * part, width), bf16)],
    )(place, *halves, *handed, right_root)
    back = local(last_strip_kernel, [smem] + [vmem] * 4, vmem, shape((owners, part, wide), bf16))(
        place, last, right_root, prec, square
    )
    back = lax.all_to_all(back, "fsdp", 0, 0, tiled=True)

    tiles = blocks * (width // 2 // LANES) + 2
    mine = local(select_kernel, [smem, vmem], vmem, shape((tiles, part, LANES), bf16))(block_slot, back)
    near = exchange(mine, NEAR)
    far = exchange(mine, FAR)
    opposite = exchange(near, FAR)
    own = [mine, near, far, opposite]
    other = [twin(x) for x in (mine, far, near, opposite)]
    return local(
        functools.partial(finish_kernel, entries=height * width),
        [smem] + [vmem] * 8,
        pl.BlockSpec(memory_space=pl.ANY),
        shape((mats, rows, full), bf16),
        [
            pltpu.VMEM((mats, rows, full), bf16),
            pltpu.VMEM((blocks, part, LANES), f32),
            pltpu.SemaphoreType.DMA((mats, 2)),
        ],
    )(place, *own, *other)


def solution(mesh):
    in_specs = (P("replica", None, "fsdp", None), P("fsdp", None, None), P("fsdp", None, None), P())
    return jax.shard_map(
        on_device, mesh=mesh, in_specs=in_specs, out_specs=P(None, "fsdp", None), check_vma=False
    )
```

```python
import functools
import jax
import jax.numpy as jnp
from jax import lax
from jax.experimental import pallas as pl
from jax.experimental.pallas import tpu as pltpu
from jax.sharding import PartitionSpec as P

EPSILON = 1e-06
LANES = 128
TERMS = 6
MIB = 1024 * 1024
VMEM_BYTES = 24 * MIB
bf16, f32 = jnp.bfloat16, jnp.float32

SELF, NEAR, FAR, OPPOSITE = range(4)
ORDER = (SELF, OPPOSITE, NEAR, FAR)
TWIN_ORDER = (SELF, OPPOSITE, FAR, NEAR)
LAST = NEAR


def masks(core):
    return 0, 1 + 2 * core, 3 - 2 * core, 2


def chip(place, relative):
    return lax.bitwise_xor(place[0] // 2, jnp.int32(masks(lax.rem(place[0], 2))[relative]))


def strip_index(place, relative, core):
    return 2 * chip(place, relative) + core


def together(copies):
    copies = list(copies)
    for copy in copies:
        copy.start()
    for copy in copies:
        copy.wait()


def send_kernel(place, grads_ref, send_ref, arrived, *, kinds):
    other = 1 - lax.rem(place[0], 2)
    order = (SELF, FAR, NEAR, OPPOSITE)
    together(
        pltpu.make_async_copy(
            grads_ref.at[:, :, :, strip_index(place, order[k], other)], send_ref.at[n], arrived.at[n]
        )
        for n, k in enumerate(kinds)
    )


def pair_sum_kernel(place, grads_ref, got_ref, *sum_refs, kinds):
    core = lax.rem(place[0], 2)
    for n, (k, sum_ref) in enumerate(zip(kinds, sum_refs)):
        piece = grads_ref[:, :, :, strip_index(place, k, core)]
        sum_ref[...] = (piece.astype(f32) + got_ref[n].astype(f32)).astype(bf16)


def add_kernel(x_ref, y_ref, out_ref):
    out_ref[...] = (x_ref[...].astype(f32) + y_ref[...].astype(f32)).astype(out_ref.dtype)


def route_kernel(slot, *refs):
    *terms, out_ref = refs
    slots = out_ref.shape[1]
    cols = terms[0].shape[2]
    out_ref[...] = jnp.zeros_like(out_ref)
    for m in range(terms[0].shape[0]):
        for j in range(cols):
            q = slot[m * cols + j]
            total = sum(term[m, :, j].astype(f32) for term in terms)
            out_ref[q // slots, lax.rem(q, slots)] = total.reshape(out_ref.shape[2:]).astype(bf16)


def left_kernel(place, left_ref, block_ref, *out_refs):
    *half_refs, scratch = out_refs
    owners, slots, rows, strip = block_ref.shape
    for s in range(slots):
        block = block_ref[:, s].reshape(owners * rows, strip)
        half = jnp.dot(left_ref[s], block, preferred_element_type=f32)
        scratch[s] = half.reshape(scratch.shape[1:])
        for k, half_ref in zip(ORDER, half_refs):
            half_ref[s] = scratch[s, :, chip(place, k)].reshape(half_ref.shape[1:]).astype(bf16)


def split3(x):
    a = x.astype(bf16).astype(f32)
    b = (x - a).astype(bf16).astype(f32)
    return a, b, x - a - b


def right_columns(place, right_ref):
    width = right_ref.shape[2] // 2
    return pl.ds(pl.multiple_of(lax.rem(place[0], 2) * width, width), width)


def strip_lines(place, relative, core, strip):
    return pl.ds(pl.multiple_of(strip_index(place, relative, core) * strip, strip), strip)


def right_kernel(place, *refs):
    *half_refs, block_ref, right_ref, prec_ref, square_ref, half_scratch = refs
    slots, _, strip = half_refs[0].shape
    core = lax.rem(place[0], 2)
    known = [(core, k) for k in ORDER] + [(1 - core, k) for k in ORDER if k != LAST]
    for s in range(slots):
        half_scratch[s, :, strip_lines(place, LAST, 1 - core, strip)] = jnp.zeros(half_refs[0].shape[1:], bf16)
        for half_ref, (c, k) in zip(half_refs, known):
            half_scratch[s, :, strip_lines(place, k, c, strip)] = half_ref[s]
        prec_ref[s] = jnp.dot(
            half_scratch[s], right_ref[s, :, right_columns(place, right_ref)], preferred_element_type=f32
        )
        block = block_ref[:, s].astype(f32)
        square = jnp.sum(block * block, axis=(0, 1))
        square = jnp.sum(square.reshape(1, strip), axis=1, keepdims=True)
        square_ref[s] = jnp.broadcast_to(square, square_ref.shape[1:])


def last_strip_kernel(place, half_ref, right_ref, prec_ref, square_ref, back_ref):
    owners, part, wide = back_ref.shape
    slots, _, strip = half_ref.shape
    width = (wide - LANES) // slots
    lane = lax.broadcasted_iota(jnp.int32, (part, LANES), 1)
    tail = jnp.zeros((part, LANES), f32)
    lines = strip_lines(place, LAST, 1 - lax.rem(place[0], 2), strip)
    for s in range(slots):
        root = right_ref[s, lines, right_columns(place, right_ref)]
        prec = prec_ref[s] + jnp.dot(half_ref[s], root, preferred_element_type=f32)
        back_ref[:, :, s * width : (s + 1) * width] = prec.reshape(owners, part, width).astype(bf16)
        prec_square = jnp.broadcast_to(jnp.sum(prec * prec, keepdims=True), (part, LANES))
        for k, term in enumerate(split3(square_ref[s]) + split3(prec_square)):
            tail = jnp.where(lane == TERMS * s + k, term, tail)
    back_ref[:, :, slots * width :] = jnp.broadcast_to(tail[None], (owners, part, LANES)).astype(bf16)


def select_kernel(slot, back_ref, tiles_ref):
    part, wide = back_ref.shape[1:]
    width = (wide - LANES) // 2
    each = width // LANES
    blocks = (tiles_ref.shape[0] - 2) // each
    lane = lax.broadcasted_iota(jnp.int32, (part, LANES), 1)
    line = lax.broadcasted_iota(jnp.int32, (part, LANES), 0)
    terms = [jnp.zeros((part, LANES), f32)] * 2
    for b in range(blocks):
        q, h, pair = slot[b], b % 2, b // 2
        s = lax.rem(q, 2)
        for t in range(each):
            columns = pl.ds(pl.multiple_of(s * width + t * LANES, LANES), LANES)
            tiles_ref[b * each + t] = back_ref[q // 2, :, columns]
        tail = back_ref[q // 2, :, 2 * width :].astype(f32)
        tail = jnp.where(s == h, tail, pltpu.roll(tail, TERMS if h else LANES - TERMS, 1))
        here = (line == pair % part) & (lane >= TERMS * h) & (lane < TERMS * (h + 1))
        terms[pair // part] = jnp.where(here, tail, terms[pair // part])
    for n in range(2):
        tiles_ref[blocks * each + n] = terms[n].astype(bf16)


def finish_kernel(place, *refs, entries):
    own_refs, twin_refs = refs[:4], refs[4:8]
    out_ref, ready, ratios, written = refs[8:]
    part = own_refs[0].shape[1]
    mats, rows, full = ready.shape
    blocks = ratios.shape[0]
    each = (own_refs[0].shape[0] - 2) // blocks
    count = blocks // mats
    lane = lax.broadcasted_iota(jnp.int32, (part, LANES), 1)
    for n in range(2):
        tail = sum(ref[blocks * each + n].astype(f32) for ref in own_refs + twin_refs)
        for h in range(2):
            block_square, prec_square = [
                jnp.sum(jnp.where((lane >= start) & (lane < start + 3), tail, 0.0), axis=1, keepdims=True)
                for start in (TERMS * h, TERMS * h + 3)
            ]
            ratio = jnp.sqrt(block_square / entries + EPSILON) / jnp.sqrt(prec_square / entries + EPSILON)
            for line in range(part):
                ratios[2 * (n * part + line) + h] = jnp.broadcast_to(ratio[line : line + 1], (part, LANES))

    def emit(m, core, odd):
        couples = ((SELF, FAR), (OPPOSITE, NEAR)) if core else ((SELF, NEAR), (OPPOSITE, FAR))
        for couple in couples:
            side = chip(place, couple[0]) // 2
            at = lines(side)
            for j in range(count):
                b = m * count + j
                for refs, c in ((own_refs, core), (twin_refs, 1 - core)):
                    for t in range(each):
                        tiles = [
                            refs[k][b * each + t].astype(f32) * ratios[b] for k in (couple[::-1] if odd else couple)
                        ]
                        columns = pl.ds(((2 * j + c) * each + t) * LANES, LANES)
                        ready[m, at, columns] = jnp.concatenate(tiles, 0).astype(bf16)
            write(m, side).start()

    def lines(side):
        return pl.ds(pl.multiple_of(side * 2 * part, 2 * part), 2 * part)

    def write(m, side):
        return pltpu.make_async_copy(ready.at[m, lines(side)], out_ref.at[m, lines(side)], written.at[m, side])

    @pl.loop(0, mats)
    def _(m):
        for core in range(2):
            for odd in range(2):
                here = (lax.rem(place[0], 2) == core) & (lax.rem(place[0] // 2, 2) == odd)
                pl.when(here)(functools.partial(emit, m, core, odd))

    for m in range(mats):
        for side in range(2):
            write(m, side).wait()


def on_device(grads, left_root, right_root, block_slot):
    owners = lax.axis_size("fsdp")
    reps = lax.axis_size("replica")
    slots, height, width = left_root.shape[0], left_root.shape[1], right_root.shape[1]
    _, mats, rows, full = grads.shape
    cols = full // width
    blocks = mats * cols
    strip = width // reps
    part = rows // 4
    shape = jax.ShapeDtypeStruct

    place = lax.axis_index("replica").reshape(1).astype(jnp.int32)
    def twin(x):
        return lax.ppermute(x, "replica", [(i, i ^ 1) for i in range(reps)])

    def exchange(x, relative):
        perm = [(i, i ^ (2 * masks(i % 2)[relative])) for i in range(reps)]
        return lax.ppermute(x, "replica", perm)

    group = 8
    tiles = grads.reshape(mats, rows // group, group, cols, reps, strip).transpose(0, 1, 3, 4, 2, 5)

    def strips(*n):
        return shape((*n, mats, rows // group, cols, group, strip), bf16)

    def local(kernel, in_specs, out_specs, out_shape, scratch_shapes=()):
        return pl.pallas_call(
            kernel,
            in_specs=in_specs,
            out_specs=out_specs,
            out_shape=out_shape,
            scratch_shapes=scratch_shapes,
            compiler_params=pltpu.CompilerParams(vmem_limit_bytes=VMEM_BYTES),
        )

    smem, vmem = pl.BlockSpec(memory_space=pltpu.SMEM), pl.BlockSpec(memory_space=pltpu.VMEM)
    sums = {}
    for kinds in ((OPPOSITE, NEAR), (SELF, FAR)):
        send = local(
            functools.partial(send_kernel, kinds=kinds),
            [smem, pl.BlockSpec(memory_space=pl.ANY)],
            vmem,
            strips(2),
            [pltpu.SemaphoreType.DMA((2,))],
        )(place, pltpu.with_memory_space_constraint(tiles, pltpu.HBM))
        got = twin(send)
        found = local(
            functools.partial(pair_sum_kernel, kinds=kinds), [smem, vmem, vmem], [vmem] * 2, [strips()] * 2
        )(place, tiles, got)
        sums.update(zip(kinds, found))

    onward = exchange(sums[OPPOSITE], NEAR)
    direct = exchange(sums[NEAR], NEAR)
    passed = local(add_kernel, [vmem] * 2, vmem, strips())(sums[FAR], onward)
    last = exchange(passed, FAR)

    known = local(add_kernel, [vmem] * 2, vmem, shape(direct.shape, f32))(sums[SELF], direct)
    outgoing = local(route_kernel, [smem] + [vmem] * 2, vmem, shape((owners, slots, rows, strip), bf16))(
        block_slot, known, last
    )
    incoming = lax.all_to_all(outgoing, "fsdp", 0, 0, tiled=True)

    half_shape = shape((slots, owners * part, strip), bf16)
    halves = local(
        left_kernel,
        [smem, vmem, vmem],
        [vmem] * 4,
        [half_shape] * 4,
        [pltpu.VMEM((slots, owners, 4, part, strip), f32)],
    )(place, left_root, incoming)
    halves = [half if k == SELF else exchange(half, k) for k, half in zip(ORDER, halves)]
    handed = [twin(halves[ORDER.index(k)]) for k in TWIN_ORDER]
    wide = width + LANES
    last = handed.pop(ORDER.index(LAST))
    prec, square = local(
        right_kernel,
        [smem] + [vmem] * 9,
        [vmem] * 2,
        [shape((slots, owners * part, width // 2), f32), shape((slots, part, LANES), f32)],
        [pltpu.VMEM((slots, owners * part, width), bf16)],
    )(place, *halves, *handed, incoming, right_root)
    back = local(last_strip_kernel, [smem] + [vmem] * 4, vmem, shape((owners, part, wide), bf16))(
        place, last, right_root, prec, square
    )
    back = lax.all_to_all(back, "fsdp", 0, 0, tiled=True)

    tiles = blocks * (width // 2 // LANES) + 2
    mine = local(select_kernel, [smem, vmem], vmem, shape((tiles, part, LANES), bf16))(block_slot, back)
    near = exchange(mine, NEAR)
    far = exchange(mine, FAR)
    opposite = exchange(near, FAR)
    own = [mine, near, far, opposite]
    other = [twin(x) for x in (mine, far, near, opposite)]
    return local(
        functools.partial(finish_kernel, entries=height * width),
        [smem] + [vmem] * 8,
        pl.BlockSpec(memory_space=pl.ANY),
        shape((mats, rows, full), bf16),
        [
            pltpu.VMEM((mats, rows, full), bf16),
            pltpu.VMEM((blocks, part, LANES), f32),
            pltpu.SemaphoreType.DMA((mats, 2)),
        ],
    )(place, *own, *other)


def solution(mesh):
    in_specs = (P("replica", None, "fsdp", None), P("fsdp", None, None), P("fsdp", None, None), P())
    return jax.shard_map(
        on_device, mesh=mesh, in_specs=in_specs, out_specs=P(None, "fsdp", None), check_vma=False
    )
```

```python
import functools
import jax
import jax.numpy as jnp
from jax import lax
from jax.experimental import pallas as pl
from jax.experimental.pallas import tpu as pltpu
from jax.sharding import PartitionSpec as P

EPSILON = 1e-06
LANES = 128
TERMS = 6
MIB = 1024 * 1024
VMEM_BYTES = 24 * MIB
bf16, f32 = jnp.bfloat16, jnp.float32

SELF, NEAR, FAR, OPPOSITE = range(4)
ORDER = (SELF, OPPOSITE, NEAR, FAR)
TWIN_ORDER = (SELF, OPPOSITE, FAR, NEAR)


def masks(core):
    return 0, 1 + 2 * core, 3 - 2 * core, 2


def chip(place, relative):
    return lax.bitwise_xor(place[0] // 2, jnp.int32(masks(lax.rem(place[0], 2))[relative]))


def strip_columns(place, relative, core, j, width, strip):
    index = 2 * chip(place, relative) + core
    return pl.ds(pl.multiple_of(j * width + index * strip, strip), strip)


def together(copies):
    copies = list(copies)
    for copy in copies:
        copy.start()
    for copy in copies:
        copy.wait()


def send_kernel(place, grads_ref, send_ref, arrived, *, kinds, cols, width, strip):
    other = 1 - lax.rem(place[0], 2)
    order = (SELF, FAR, NEAR, OPPOSITE)
    together(
        pltpu.make_async_copy(
            grads_ref.at[0, :, :, strip_columns(place, order[k], other, j, width, strip)],
            send_ref.at[n, :, j],
            arrived.at[n * cols + j],
        )
        for n, k in enumerate(kinds)
        for j in range(cols)
    )


def pair_sum_kernel(place, grads_ref, got_ref, *sum_refs, kinds, cols, width, strip):
    core = lax.rem(place[0], 2)
    for n, (k, sum_ref) in enumerate(zip(kinds, sum_refs)):
        for m in range(grads_ref.shape[1]):
            for j in range(cols):
                piece = grads_ref[0, m, :, strip_columns(place, k, core, j, width, strip)]
                sum_ref[m, j] = (piece.astype(f32) + got_ref[n, m, j].astype(f32)).astype(bf16)


def add_kernel(x_ref, y_ref, out_ref):
    out_ref[...] = (x_ref[...].astype(f32) + y_ref[...].astype(f32)).astype(bf16)


def route_kernel(slot, *refs):
    *terms, out_ref = refs
    slots = out_ref.shape[1]
    cols = terms[0].shape[1]
    out_ref[...] = jnp.zeros_like(out_ref)
    for m in range(terms[0].shape[0]):
        for j in range(cols):
            q = slot[m * cols + j]
            total = sum(term[m, j].astype(f32) for term in terms)
            out_ref[q // slots, lax.rem(q, slots)] = total.astype(bf16)


def left_kernel(place, left_ref, block_ref, *out_refs):
    *half_refs, square_ref, scratch = out_refs
    owners, slots, rows, strip = block_ref.shape
    for s in range(slots):
        block = block_ref[:, s].reshape(owners * rows, strip)
        wide = block.astype(f32)
        square_ref[s] = jnp.broadcast_to(jnp.sum(wide * wide, keepdims=True), square_ref.shape[1:])
        half = jnp.dot(left_ref[s], block, preferred_element_type=f32)
        scratch[s] = half.reshape(scratch.shape[1:])
        for k, half_ref in zip(ORDER, half_refs):
            half_ref[s] = scratch[s, :, chip(place, k)].reshape(half_ref.shape[1:]).astype(bf16)


def split3(x):
    a = x.astype(bf16).astype(f32)
    b = (x - a).astype(bf16).astype(f32)
    return a, b, x - a - b


def right_kernel(place, *refs):
    own_refs, twin_refs = refs[:4], refs[4:8]
    right_ref, square_ref, back_ref, half_scratch = refs[8:]
    owners, part, wide = back_ref.shape
    slots = right_ref.shape[0]
    width = (wide - LANES) // slots
    strip = own_refs[0].shape[2]
    core = lax.rem(place[0], 2)
    lane = lax.broadcasted_iota(jnp.int32, (part, LANES), 1)
    tail = jnp.zeros((part, LANES), f32)
    for s in range(slots):
        for half_refs, c in ((own_refs, core), (twin_refs, 1 - core)):
            for k, half_ref in zip(ORDER, half_refs):
                r = 2 * chip(place, k) + c
                half_scratch[s, :, pl.ds(pl.multiple_of(r * strip, strip), strip)] = half_ref[s]
        columns = pl.ds(pl.multiple_of(core * width, width), width)
        prec = jnp.dot(half_scratch[s], right_ref[s, :, columns], preferred_element_type=f32)
        back_ref[:, :, s * width : (s + 1) * width] = prec.reshape(owners, part, width).astype(bf16)
        prec_square = jnp.broadcast_to(jnp.sum(prec * prec, keepdims=True), (part, LANES))
        for k, term in enumerate(split3(square_ref[s]) + split3(prec_square)):
            tail = jnp.where(lane == TERMS * s + k, term, tail)
    back_ref[:, :, slots * width :] = jnp.broadcast_to(tail[None], (owners, part, LANES)).astype(bf16)


def select_kernel(slot, back_ref, tiles_ref):
    part, wide = back_ref.shape[1:]
    width = (wide - LANES) // 2
    each = width // LANES
    blocks = (tiles_ref.shape[0] - 2) // each
    lane = lax.broadcasted_iota(jnp.int32, (part, LANES), 1)
    line = lax.broadcasted_iota(jnp.int32, (part, LANES), 0)
    terms = [jnp.zeros((part, LANES), f32)] * 2
    for b in range(blocks):
        q, h, pair = slot[b], b % 2, b // 2
        s = lax.rem(q, 2)
        for t in range(each):
            columns = pl.ds(pl.multiple_of(s * width + t * LANES, LANES), LANES)
            tiles_ref[b * each + t] = back_ref[q // 2, :, columns]
        tail = back_ref[q // 2, :, 2 * width :].astype(f32)
        tail = jnp.where(s == h, tail, pltpu.roll(tail, TERMS if h else LANES - TERMS, 1))
        here = (line == pair % part) & (lane >= TERMS * h) & (lane < TERMS * (h + 1))
        terms[pair // part] = jnp.where(here, tail, terms[pair // part])
    for n in range(2):
        tiles_ref[blocks * each + n] = terms[n].astype(bf16)


def finish_kernel(place, *refs, entries):
    own_refs, twin_refs = refs[:4], refs[4:8]
    out_ref, ready, ratios, written = refs[8:]
    part = own_refs[0].shape[1]
    mats, rows, full = ready.shape
    blocks = ratios.shape[0]
    each = (own_refs[0].shape[0] - 2) // blocks
    count = blocks // mats
    lane = lax.broadcasted_iota(jnp.int32, (part, LANES), 1)
    for n in range(2):
        tail = sum(ref[blocks * each + n].astype(f32) for ref in own_refs + twin_refs)
        for h in range(2):
            block_square, prec_square = [
                jnp.sum(jnp.where((lane >= start) & (lane < start + 3), tail, 0.0), axis=1, keepdims=True)
                for start in (TERMS * h, TERMS * h + 3)
            ]
            ratio = jnp.sqrt(block_square / entries + EPSILON) / jnp.sqrt(prec_square / entries + EPSILON)
            for line in range(part):
                ratios[2 * (n * part + line) + h] = jnp.broadcast_to(ratio[line : line + 1], (part, LANES))

    def emit(m, core, odd):
        couples = ((SELF, FAR), (OPPOSITE, NEAR)) if core else ((SELF, NEAR), (OPPOSITE, FAR))
        for couple in couples:
            at = pl.ds(pl.multiple_of(chip(place, couple[0]) // 2 * 2 * part, 2 * part), 2 * part)
            for j in range(count):
                b = m * count + j
                for refs, c in ((own_refs, core), (twin_refs, 1 - core)):
                    for t in range(each):
                        tiles = [
                            refs[k][b * each + t].astype(f32) * ratios[b] for k in (couple[::-1] if odd else couple)
                        ]
                        columns = pl.ds(((2 * j + c) * each + t) * LANES, LANES)
                        ready[m, at, columns] = jnp.concatenate(tiles, 0).astype(bf16)

    def write(m):
        return pltpu.make_async_copy(ready.at[m], out_ref.at[m], written.at[m])

    @pl.loop(0, mats)
    def _(m):
        for core in range(2):
            for odd in range(2):
                here = (lax.rem(place[0], 2) == core) & (lax.rem(place[0] // 2, 2) == odd)
                pl.when(here)(functools.partial(emit, m, core, odd))
        write(m).start()

    for m in range(mats):
        write(m).wait()


def on_device(grads, left_root, right_root, block_slot):
    owners = lax.axis_size("fsdp")
    reps = lax.axis_size("replica")
    slots, height, width = left_root.shape[0], left_root.shape[1], right_root.shape[1]
    _, mats, rows, full = grads.shape
    cols = full // width
    blocks = mats * cols
    strip = width // reps
    part = rows // 4
    shape = jax.ShapeDtypeStruct

    place = lax.axis_index("replica").reshape(1).astype(jnp.int32)
    def twin(x):
        return lax.ppermute(x, "replica", [(i, i ^ 1) for i in range(reps)])

    def exchange(x, relative):
        perm = [(i, i ^ (2 * masks(i % 2)[relative])) for i in range(reps)]
        return lax.ppermute(x, "replica", perm)

    sizes = dict(cols=cols, width=width, strip=strip)
    def strips(*n):
        return shape((*n, mats, cols, rows, strip), bf16)

    def local(kernel, in_specs, out_specs, out_shape, scratch_shapes=()):
        return pl.pallas_call(
            kernel,
            in_specs=in_specs,
            out_specs=out_specs,
            out_shape=out_shape,
            scratch_shapes=scratch_shapes,
            compiler_params=pltpu.CompilerParams(vmem_limit_bytes=VMEM_BYTES),
        )

    smem, vmem = pl.BlockSpec(memory_space=pltpu.SMEM), pl.BlockSpec(memory_space=pltpu.VMEM)
    sums = {}
    for kinds in ((OPPOSITE, NEAR), (SELF, FAR)):
        send = local(
            functools.partial(send_kernel, kinds=kinds, **sizes),
            [smem, pl.BlockSpec(memory_space=pl.ANY)],
            vmem,
            strips(2),
            [pltpu.SemaphoreType.DMA((2 * cols,))],
        )(place, pltpu.with_memory_space_constraint(grads, pltpu.HBM))
        got = twin(send)
        found = local(
            functools.partial(pair_sum_kernel, kinds=kinds, **sizes), [smem, vmem, vmem], [vmem] * 2, [strips()] * 2
        )(place, grads, got)
        sums.update(zip(kinds, found))

    onward = exchange(sums[OPPOSITE], NEAR)
    direct = exchange(sums[NEAR], NEAR)
    passed = local(add_kernel, [vmem] * 2, vmem, strips())(sums[FAR], onward)
    last = exchange(passed, FAR)

    outgoing = local(route_kernel, [smem] + [vmem] * 3, vmem, shape((owners, slots, rows, strip), bf16))(
        block_slot, sums[SELF], direct, last
    )
    incoming = lax.all_to_all(outgoing, "fsdp", 0, 0, tiled=True)

    half_shape = shape((slots, owners * part, strip), bf16)
    *halves, square = local(
        left_kernel,
        [smem, vmem, vmem],
        [vmem] * 5,
        [half_shape] * 4 + [shape((slots, part, LANES), f32)],
        [pltpu.VMEM((slots, owners, 4, part, strip), f32)],
    )(place, left_root, incoming)
    halves = [half if k == SELF else exchange(half, k) for k, half in zip(ORDER, halves)]
    handed = [twin(halves[ORDER.index(k)]) for k in TWIN_ORDER]
    wide = width + LANES
    back = local(
        right_kernel,
        [smem] + [vmem] * 10,
        vmem,
        shape((owners, part, wide), bf16),
        [pltpu.VMEM((slots, owners * part, width), bf16)],
    )(place, *halves, *handed, right_root, square)
    back = lax.all_to_all(back, "fsdp", 0, 0, tiled=True)

    tiles = blocks * (width // 2 // LANES) + 2
    mine = local(select_kernel, [smem, vmem], vmem, shape((tiles, part, LANES), bf16))(block_slot, back)
    near = exchange(mine, NEAR)
    far = exchange(mine, FAR)
    opposite = exchange(far, NEAR)
    own = [mine, near, far, opposite]
    other = [twin(x) for x in (mine, far, near, opposite)]
    return local(
        functools.partial(finish_kernel, entries=height * width),
        [smem] + [vmem] * 8,
        pl.BlockSpec(memory_space=pl.ANY),
        shape((mats, rows, full), bf16),
        [
            pltpu.VMEM((mats, rows, full), bf16),
            pltpu.VMEM((blocks, part, LANES), f32),
            pltpu.SemaphoreType.DMA((mats,)),
        ],
    )(place, *own, *other)


def solution(mesh):
    in_specs = (P("replica", None, "fsdp", None), P("fsdp", None, None), P("fsdp", None, None), P())
    return jax.shard_map(
        on_device, mesh=mesh, in_specs=in_specs, out_specs=P(None, "fsdp", None), check_vma=False
    )
```

```python
import functools
import jax
import jax.numpy as jnp
from jax import lax
from jax.experimental import pallas as pl
from jax.experimental.pallas import tpu as pltpu
from jax.sharding import PartitionSpec as P

EPSILON = 1e-06
LANES = 128
TERMS = 6
MIB = 1024 * 1024
VMEM_BYTES = 24 * MIB
bf16, f32 = jnp.bfloat16, jnp.float32

SELF, NEAR, FAR, OPPOSITE = range(4)
ORDER = (SELF, OPPOSITE, NEAR, FAR)
TWIN_ORDER = (SELF, OPPOSITE, FAR, NEAR)


def masks(core):
    return 0, 1 + 2 * core, 3 - 2 * core, 2


def chip(place, relative):
    return lax.bitwise_xor(place[0] // 2, jnp.int32(masks(lax.rem(place[0], 2))[relative]))


def strip_columns(place, relative, core, j, width, strip):
    index = 2 * chip(place, relative) + core
    return pl.ds(pl.multiple_of(j * width + index * strip, strip), strip)


def together(copies):
    copies = list(copies)
    for copy in copies:
        copy.start()
    for copy in copies:
        copy.wait()


def send_kernel(place, grads_ref, send_ref, arrived, *, kinds, cols, width, strip):
    other = 1 - lax.rem(place[0], 2)
    order = (SELF, FAR, NEAR, OPPOSITE)
    together(
        pltpu.make_async_copy(
            grads_ref.at[0, :, :, strip_columns(place, order[k], other, j, width, strip)],
            send_ref.at[n, :, j],
            arrived.at[n * cols + j],
        )
        for n, k in enumerate(kinds)
        for j in range(cols)
    )


def pair_sum_kernel(place, grads_ref, got_ref, *sum_refs, kinds, cols, width, strip):
    core = lax.rem(place[0], 2)
    for n, (k, sum_ref) in enumerate(zip(kinds, sum_refs)):
        for m in range(grads_ref.shape[1]):
            for j in range(cols):
                piece = grads_ref[0, m, :, strip_columns(place, k, core, j, width, strip)]
                sum_ref[m, j] = (piece.astype(f32) + got_ref[n, m, j].astype(f32)).astype(bf16)


def add_kernel(x_ref, y_ref, out_ref):
    out_ref[...] = (x_ref[...].astype(f32) + y_ref[...].astype(f32)).astype(bf16)


def route_kernel(slot, *refs):
    *terms, out_ref = refs
    slots = out_ref.shape[1]
    cols = terms[0].shape[1]
    out_ref[...] = jnp.zeros_like(out_ref)
    for m in range(terms[0].shape[0]):
        for j in range(cols):
            q = slot[m * cols + j]
            total = sum(term[m, j].astype(f32) for term in terms)
            out_ref[q // slots, lax.rem(q, slots)] = total.astype(bf16)


def left_kernel(place, left_ref, block_ref, *out_refs):
    *half_refs, square_ref, scratch = out_refs
    owners, slots, rows, strip = block_ref.shape
    for s in range(slots):
        block = block_ref[:, s].reshape(owners * rows, strip)
        wide = block.astype(f32)
        square_ref[s] = jnp.broadcast_to(jnp.sum(wide * wide, keepdims=True), square_ref.shape[1:])
        half = jnp.dot(left_ref[s], block, preferred_element_type=f32)
        scratch[s] = half.reshape(scratch.shape[1:])
        for k, half_ref in zip(ORDER, half_refs):
            half_ref[s] = scratch[s, :, chip(place, k)].reshape(half_ref.shape[1:]).astype(bf16)


def split3(x):
    a = x.astype(bf16).astype(f32)
    b = (x - a).astype(bf16).astype(f32)
    return a, b, x - a - b


def right_kernel(place, *refs):
    own_refs, twin_refs = refs[:4], refs[4:8]
    right_ref, square_ref, back_ref, half_scratch = refs[8:]
    owners, part, wide = back_ref.shape
    slots = right_ref.shape[0]
    width = (wide - LANES) // slots
    strip = own_refs[0].shape[2]
    core = lax.rem(place[0], 2)
    lane = lax.broadcasted_iota(jnp.int32, (part, LANES), 1)
    tail = jnp.zeros((part, LANES), f32)
    for s in range(slots):
        for half_refs, c in ((own_refs, core), (twin_refs, 1 - core)):
            for k, half_ref in zip(ORDER, half_refs):
                r = 2 * chip(place, k) + c
                half_scratch[s, :, pl.ds(pl.multiple_of(r * strip, strip), strip)] = half_ref[s]
        columns = pl.ds(pl.multiple_of(core * width, width), width)
        prec = jnp.dot(half_scratch[s], right_ref[s, :, columns], preferred_element_type=f32)
        back_ref[:, :, s * width : (s + 1) * width] = prec.reshape(owners, part, width).astype(bf16)
        prec_square = jnp.broadcast_to(jnp.sum(prec * prec, keepdims=True), (part, LANES))
        for k, term in enumerate(split3(square_ref[s]) + split3(prec_square)):
            tail = jnp.where(lane == TERMS * s + k, term, tail)
    back_ref[:, :, slots * width :] = jnp.broadcast_to(tail[None], (owners, part, LANES)).astype(bf16)


def select_kernel(slot, back_ref, tiles_ref):
    part, wide = back_ref.shape[1:]
    width = (wide - LANES) // 2
    each = width // LANES
    blocks = slot.shape[0]
    line = lax.broadcasted_iota(jnp.int32, (part, LANES), 0)
    for n in range(blocks // part):
        terms = jnp.zeros((part, LANES), f32)
        for b in range(n * part, (n + 1) * part):
            q = slot[b]
            s = lax.rem(q, 2)
            for t in range(each):
                columns = pl.ds(pl.multiple_of(s * width + t * LANES, LANES), LANES)
                tiles_ref[b * each + t] = back_ref[q // 2, :, columns]
            terms = jnp.where(line == b % part, back_ref[q // 2, :, 2 * width :].astype(f32), terms)
        tiles_ref[blocks * each + n] = terms.astype(bf16)


def finish_kernel(place, slot, *refs, entries):
    own_refs, twin_refs = refs[:4], refs[4:8]
    out_ref, ready, ratios, written = refs[8:]
    part = own_refs[0].shape[1]
    mats, rows, full = ready.shape
    blocks = ratios.shape[0]
    each = (own_refs[0].shape[0] - blocks // part) // blocks
    count = blocks // mats
    lane = lax.broadcasted_iota(jnp.int32, (part, LANES), 1)
    for n in range(blocks // part):
        tail = sum(ref[blocks * each + n].astype(f32) for ref in own_refs + twin_refs)
        found = []
        for h in range(2):
            block_square, prec_square = [
                jnp.sum(jnp.where((lane >= start) & (lane < start + 3), tail, 0.0), axis=1, keepdims=True)
                for start in (TERMS * h, TERMS * h + 3)
            ]
            found.append(jnp.sqrt(block_square / entries + EPSILON) / jnp.sqrt(prec_square / entries + EPSILON))
        for line in range(part):
            b = n * part + line
            first, second = (jnp.broadcast_to(ratio[line : line + 1], (part, LANES)) for ratio in found)
            ratios[b] = jnp.where(lax.rem(slot[b], 2) == 0, first, second)

    def emit(m, core, odd):
        couples = ((SELF, FAR), (OPPOSITE, NEAR)) if core else ((SELF, NEAR), (OPPOSITE, FAR))
        for couple in couples:
            at = pl.ds(pl.multiple_of(chip(place, couple[0]) // 2 * 2 * part, 2 * part), 2 * part)
            for j in range(count):
                b = m * count + j
                for refs, c in ((own_refs, core), (twin_refs, 1 - core)):
                    for t in range(each):
                        tiles = [
                            refs[k][b * each + t].astype(f32) * ratios[b] for k in (couple[::-1] if odd else couple)
                        ]
                        columns = pl.ds(((2 * j + c) * each + t) * LANES, LANES)
                        ready[m, at, columns] = jnp.concatenate(tiles, 0).astype(bf16)

    def write(m):
        return pltpu.make_async_copy(ready.at[m], out_ref.at[m], written.at[m])

    @pl.loop(0, mats)
    def _(m):
        for core in range(2):
            for odd in range(2):
                here = (lax.rem(place[0], 2) == core) & (lax.rem(place[0] // 2, 2) == odd)
                pl.when(here)(functools.partial(emit, m, core, odd))
        write(m).start()

    for m in range(mats):
        write(m).wait()


def on_device(grads, left_root, right_root, block_slot):
    owners = lax.axis_size("fsdp")
    reps = lax.axis_size("replica")
    slots, height, width = left_root.shape[0], left_root.shape[1], right_root.shape[1]
    _, mats, rows, full = grads.shape
    cols = full // width
    blocks = mats * cols
    strip = width // reps
    part = rows // 4
    shape = jax.ShapeDtypeStruct

    place = lax.axis_index("replica").reshape(1).astype(jnp.int32)
    def twin(x):
        return lax.ppermute(x, "replica", [(i, i ^ 1) for i in range(reps)])

    def exchange(x, relative):
        perm = [(i, i ^ (2 * masks(i % 2)[relative])) for i in range(reps)]
        return lax.ppermute(x, "replica", perm)

    sizes = dict(cols=cols, width=width, strip=strip)
    def strips(*n):
        return shape((*n, mats, cols, rows, strip), bf16)

    def local(kernel, in_specs, out_specs, out_shape, scratch_shapes=()):
        return pl.pallas_call(
            kernel,
            in_specs=in_specs,
            out_specs=out_specs,
            out_shape=out_shape,
            scratch_shapes=scratch_shapes,
            compiler_params=pltpu.CompilerParams(vmem_limit_bytes=VMEM_BYTES),
        )

    smem, vmem = pl.BlockSpec(memory_space=pltpu.SMEM), pl.BlockSpec(memory_space=pltpu.VMEM)
    sums = {}
    for kinds in ((OPPOSITE, NEAR), (SELF, FAR)):
        send = local(
            functools.partial(send_kernel, kinds=kinds, **sizes),
            [smem, pl.BlockSpec(memory_space=pl.ANY)],
            vmem,
            strips(2),
            [pltpu.SemaphoreType.DMA((2 * cols,))],
        )(place, pltpu.with_memory_space_constraint(grads, pltpu.HBM))
        got = twin(send)
        found = local(
            functools.partial(pair_sum_kernel, kinds=kinds, **sizes), [smem, vmem, vmem], [vmem] * 2, [strips()] * 2
        )(place, grads, got)
        sums.update(zip(kinds, found))

    onward = exchange(sums[OPPOSITE], NEAR)
    direct = exchange(sums[NEAR], NEAR)
    passed = local(add_kernel, [vmem] * 2, vmem, strips())(sums[FAR], onward)
    last = exchange(passed, FAR)

    outgoing = local(route_kernel, [smem] + [vmem] * 3, vmem, shape((owners, slots, rows, strip), bf16))(
        block_slot, sums[SELF], direct, last
    )
    incoming = lax.all_to_all(outgoing, "fsdp", 0, 0, tiled=True)

    half_shape = shape((slots, owners * part, strip), bf16)
    *halves, square = local(
        left_kernel,
        [smem, vmem, vmem],
        [vmem] * 5,
        [half_shape] * 4 + [shape((slots, part, LANES), f32)],
        [pltpu.VMEM((slots, owners, 4, part, strip), f32)],
    )(place, left_root, incoming)
    halves = [half if k == SELF else exchange(half, k) for k, half in zip(ORDER, halves)]
    handed = [twin(halves[ORDER.index(k)]) for k in TWIN_ORDER]
    wide = width + LANES
    back = local(
        right_kernel,
        [smem] + [vmem] * 10,
        vmem,
        shape((owners, part, wide), bf16),
        [pltpu.VMEM((slots, owners * part, width), bf16)],
    )(place, *halves, *handed, right_root, square)
    back = lax.all_to_all(back, "fsdp", 0, 0, tiled=True)

    tiles = blocks * (width // 2 // LANES) + blocks // part
    mine = local(select_kernel, [smem, vmem], vmem, shape((tiles, part, LANES), bf16))(block_slot, back)
    near = exchange(mine, NEAR)
    far = exchange(mine, FAR)
    opposite = exchange(near, FAR)
    own = [mine, near, far, opposite]
    other = [twin(x) for x in (mine, far, near, opposite)]
    return local(
        functools.partial(finish_kernel, entries=height * width),
        [smem] * 2 + [vmem] * 8,
        pl.BlockSpec(memory_space=pl.ANY),
        shape((mats, rows, full), bf16),
        [
            pltpu.VMEM((mats, rows, full), bf16),
            pltpu.VMEM((blocks, part, LANES), f32),
            pltpu.SemaphoreType.DMA((mats,)),
        ],
    )(place, block_slot, *own, *other)


def solution(mesh):
    in_specs = (P("replica", None, "fsdp", None), P("fsdp", None, None), P("fsdp", None, None), P())
    return jax.shard_map(
        on_device, mesh=mesh, in_specs=in_specs, out_specs=P(None, "fsdp", None), check_vma=False
    )
```

```python
import functools
import jax
import jax.numpy as jnp
from jax import lax
from jax.experimental import pallas as pl
from jax.experimental.pallas import tpu as pltpu
from jax.sharding import PartitionSpec as P

EPSILON = 1e-06
LANES = 128
TERMS = 6
MIB = 1024 * 1024
VMEM_BYTES = 24 * MIB
bf16, f32 = jnp.bfloat16, jnp.float32

SELF, NEAR, FAR, OPPOSITE = range(4)
ORDER = (SELF, OPPOSITE, NEAR, FAR)
TWIN_ORDER = (SELF, OPPOSITE, FAR, NEAR)
LAST = NEAR


def masks(core):
    return 0, 1 + 2 * core, 3 - 2 * core, 2


def chip(place, relative):
    return lax.bitwise_xor(place[0] // 2, jnp.int32(masks(lax.rem(place[0], 2))[relative]))


def strip_columns(place, relative, core, j, width, strip):
    index = 2 * chip(place, relative) + core
    return pl.ds(pl.multiple_of(j * width + index * strip, strip), strip)


def together(copies):
    copies = list(copies)
    for copy in copies:
        copy.start()
    for copy in copies:
        copy.wait()


def send_kernel(place, grads_ref, send_ref, arrived, *, kinds, cols, width, strip):
    other = 1 - lax.rem(place[0], 2)
    order = (SELF, FAR, NEAR, OPPOSITE)
    together(
        pltpu.make_async_copy(
            grads_ref.at[0, :, :, strip_columns(place, order[k], other, j, width, strip)],
            send_ref.at[n, :, j],
            arrived.at[n * cols + j],
        )
        for n, k in enumerate(kinds)
        for j in range(cols)
    )


def pair_sum_kernel(place, grads_ref, got_ref, *sum_refs, kinds, cols, width, strip):
    core = lax.rem(place[0], 2)
    for n, (k, sum_ref) in enumerate(zip(kinds, sum_refs)):
        for m in range(grads_ref.shape[1]):
            for j in range(cols):
                piece = grads_ref[0, m, :, strip_columns(place, k, core, j, width, strip)]
                sum_ref[m, j] = (piece.astype(f32) + got_ref[n, m, j].astype(f32)).astype(bf16)


def add_kernel(x_ref, y_ref, out_ref):
    out_ref[...] = (x_ref[...].astype(f32) + y_ref[...].astype(f32)).astype(bf16)


def route_kernel(slot, *refs):
    *terms, out_ref = refs
    slots = out_ref.shape[1]
    cols = terms[0].shape[1]
    out_ref[...] = jnp.zeros_like(out_ref)
    for m in range(terms[0].shape[0]):
        for j in range(cols):
            q = slot[m * cols + j]
            total = sum(term[m, j].astype(f32) for term in terms)
            out_ref[q // slots, lax.rem(q, slots)] = total.astype(bf16)


def left_kernel(place, left_ref, block_ref, *out_refs):
    *half_refs, square_ref, scratch = out_refs
    owners, slots, rows, strip = block_ref.shape
    for s in range(slots):
        block = block_ref[:, s].reshape(owners * rows, strip)
        wide = block.astype(f32)
        square_ref[s] = jnp.broadcast_to(jnp.sum(wide * wide, keepdims=True), square_ref.shape[1:])
        half = jnp.dot(left_ref[s], block, preferred_element_type=f32)
        scratch[s] = half.reshape(scratch.shape[1:])
        for k, half_ref in zip(ORDER, half_refs):
            half_ref[s] = scratch[s, :, chip(place, k)].reshape(half_ref.shape[1:]).astype(bf16)


def split3(x):
    a = x.astype(bf16).astype(f32)
    b = (x - a).astype(bf16).astype(f32)
    return a, b, x - a - b


def right_columns(place, right_ref):
    width = right_ref.shape[2] // 2
    return pl.ds(pl.multiple_of(lax.rem(place[0], 2) * width, width), width)


def strip_lines(place, relative, core, strip):
    return pl.ds(pl.multiple_of((2 * chip(place, relative) + core) * strip, strip), strip)


def right_kernel(place, *refs):
    *half_refs, right_ref, prec_ref, half_scratch = refs
    slots, _, strip = half_refs[0].shape
    core = lax.rem(place[0], 2)
    known = [(core, k) for k in ORDER] + [(1 - core, k) for k in ORDER if k != LAST]
    for s in range(slots):
        half_scratch[s, :, strip_lines(place, LAST, 1 - core, strip)] = jnp.zeros(half_refs[0].shape[1:], bf16)
        for half_ref, (c, k) in zip(half_refs, known):
            half_scratch[s, :, strip_lines(place, k, c, strip)] = half_ref[s]
        prec_ref[s] = jnp.dot(
            half_scratch[s], right_ref[s, :, right_columns(place, right_ref)], preferred_element_type=f32
        )


def last_strip_kernel(place, half_ref, right_ref, prec_ref, square_ref, back_ref):
    owners, part, wide = back_ref.shape
    slots, _, strip = half_ref.shape
    width = (wide - LANES) // slots
    lane = lax.broadcasted_iota(jnp.int32, (part, LANES), 1)
    tail = jnp.zeros((part, LANES), f32)
    lines = strip_lines(place, LAST, 1 - lax.rem(place[0], 2), strip)
    for s in range(slots):
        root = right_ref[s, lines, right_columns(place, right_ref)]
        prec = prec_ref[s] + jnp.dot(half_ref[s], root, preferred_element_type=f32)
        back_ref[:, :, s * width : (s + 1) * width] = prec.reshape(owners, part, width).astype(bf16)
        prec_square = jnp.broadcast_to(jnp.sum(prec * prec, keepdims=True), (part, LANES))
        for k, term in enumerate(split3(square_ref[s]) + split3(prec_square)):
            tail = jnp.where(lane == TERMS * s + k, term, tail)
    back_ref[:, :, slots * width :] = jnp.broadcast_to(tail[None], (owners, part, LANES)).astype(bf16)


def select_kernel(slot, back_ref, tiles_ref):
    part, wide = back_ref.shape[1:]
    width = (wide - LANES) // 2
    each = width // LANES
    blocks = (tiles_ref.shape[0] - 2) // each
    lane = lax.broadcasted_iota(jnp.int32, (part, LANES), 1)
    line = lax.broadcasted_iota(jnp.int32, (part, LANES), 0)
    terms = [jnp.zeros((part, LANES), f32)] * 2
    for b in range(blocks):
        q, h, pair = slot[b], b % 2, b // 2
        s = lax.rem(q, 2)
        for t in range(each):
            columns = pl.ds(pl.multiple_of(s * width + t * LANES, LANES), LANES)
            tiles_ref[b * each + t] = back_ref[q // 2, :, columns]
        tail = back_ref[q // 2, :, 2 * width :].astype(f32)
        tail = jnp.where(s == h, tail, pltpu.roll(tail, TERMS if h else LANES - TERMS, 1))
        here = (line == pair % part) & (lane >= TERMS * h) & (lane < TERMS * (h + 1))
        terms[pair // part] = jnp.where(here, tail, terms[pair // part])
    for n in range(2):
        tiles_ref[blocks * each + n] = terms[n].astype(bf16)


def finish_kernel(place, *refs, entries):
    own_refs, twin_refs = refs[:4], refs[4:8]
    out_ref, ready, ratios, written = refs[8:]
    part = own_refs[0].shape[1]
    mats, rows, full = ready.shape
    blocks = ratios.shape[0]
    each = (own_refs[0].shape[0] - 2) // blocks
    count = blocks // mats
    lane = lax.broadcasted_iota(jnp.int32, (part, LANES), 1)
    for n in range(2):
        tail = sum(ref[blocks * each + n].astype(f32) for ref in own_refs + twin_refs)
        for h in range(2):
            block_square, prec_square = [
                jnp.sum(jnp.where((lane >= start) & (lane < start + 3), tail, 0.0), axis=1, keepdims=True)
                for start in (TERMS * h, TERMS * h + 3)
            ]
            ratio = jnp.sqrt(block_square / entries + EPSILON) / jnp.sqrt(prec_square / entries + EPSILON)
            for line in range(part):
                ratios[2 * (n * part + line) + h] = jnp.broadcast_to(ratio[line : line + 1], (part, LANES))

    def emit(m, core, odd):
        couples = ((SELF, FAR), (OPPOSITE, NEAR)) if core else ((SELF, NEAR), (OPPOSITE, FAR))
        for couple in couples:
            at = pl.ds(pl.multiple_of(chip(place, couple[0]) // 2 * 2 * part, 2 * part), 2 * part)
            for j in range(count):
                b = m * count + j
                for refs, c in ((own_refs, core), (twin_refs, 1 - core)):
                    for t in range(each):
                        tiles = [
                            refs[k][b * each + t].astype(f32) * ratios[b] for k in (couple[::-1] if odd else couple)
                        ]
                        columns = pl.ds(((2 * j + c) * each + t) * LANES, LANES)
                        ready[m, at, columns] = jnp.concatenate(tiles, 0).astype(bf16)

    def write(m):
        return pltpu.make_async_copy(ready.at[m], out_ref.at[m], written.at[m])

    @pl.loop(0, mats)
    def _(m):
        for core in range(2):
            for odd in range(2):
                here = (lax.rem(place[0], 2) == core) & (lax.rem(place[0] // 2, 2) == odd)
                pl.when(here)(functools.partial(emit, m, core, odd))
        write(m).start()

    for m in range(mats):
        write(m).wait()


def on_device(grads, left_root, right_root, block_slot):
    owners = lax.axis_size("fsdp")
    reps = lax.axis_size("replica")
    slots, height, width = left_root.shape[0], left_root.shape[1], right_root.shape[1]
    _, mats, rows, full = grads.shape
    cols = full // width
    blocks = mats * cols
    strip = width // reps
    part = rows // 4
    shape = jax.ShapeDtypeStruct

    place = lax.axis_index("replica").reshape(1).astype(jnp.int32)
    def twin(x):
        return lax.ppermute(x, "replica", [(i, i ^ 1) for i in range(reps)])

    def exchange(x, relative):
        perm = [(i, i ^ (2 * masks(i % 2)[relative])) for i in range(reps)]
        return lax.ppermute(x, "replica", perm)

    sizes = dict(cols=cols, width=width, strip=strip)
    def strips(*n):
        return shape((*n, mats, cols, rows, strip), bf16)

    def local(kernel, in_specs, out_specs, out_shape, scratch_shapes=()):
        return pl.pallas_call(
            kernel,
            in_specs=in_specs,
            out_specs=out_specs,
            out_shape=out_shape,
            scratch_shapes=scratch_shapes,
            compiler_params=pltpu.CompilerParams(vmem_limit_bytes=VMEM_BYTES),
        )

    smem, vmem = pl.BlockSpec(memory_space=pltpu.SMEM), pl.BlockSpec(memory_space=pltpu.VMEM)
    sums = {}
    for kinds in ((OPPOSITE, NEAR), (SELF, FAR)):
        send = local(
            functools.partial(send_kernel, kinds=kinds, **sizes),
            [smem, pl.BlockSpec(memory_space=pl.ANY)],
            vmem,
            strips(2),
            [pltpu.SemaphoreType.DMA((2 * cols,))],
        )(place, pltpu.with_memory_space_constraint(grads, pltpu.HBM))
        got = twin(send)
        found = local(
            functools.partial(pair_sum_kernel, kinds=kinds, **sizes), [smem, vmem, vmem], [vmem] * 2, [strips()] * 2
        )(place, grads, got)
        sums.update(zip(kinds, found))

    onward = exchange(sums[OPPOSITE], NEAR)
    direct = exchange(sums[NEAR], NEAR)
    passed = local(add_kernel, [vmem] * 2, vmem, strips())(sums[FAR], onward)
    last = exchange(passed, FAR)

    outgoing = local(route_kernel, [smem] + [vmem] * 3, vmem, shape((owners, slots, rows, strip), bf16))(
        block_slot, sums[SELF], direct, last
    )
    incoming = lax.all_to_all(outgoing, "fsdp", 0, 0, tiled=True)

    half_shape = shape((slots, owners * part, strip), bf16)
    *halves, square = local(
        left_kernel,
        [smem, vmem, vmem],
        [vmem] * 5,
        [half_shape] * 4 + [shape((slots, part, LANES), f32)],
        [pltpu.VMEM((slots, owners, 4, part, strip), f32)],
    )(place, left_root, incoming)
    halves = [half if k == SELF else exchange(half, k) for k, half in zip(ORDER, halves)]
    handed = [twin(halves[ORDER.index(k)]) for k in TWIN_ORDER]
    wide = width + LANES
    last = handed.pop(ORDER.index(LAST))
    prec = local(
        right_kernel,
        [smem] + [vmem] * 8,
        vmem,
        shape((slots, owners * part, width // 2), f32),
        [pltpu.VMEM((slots, owners * part, width), bf16)],
    )(place, *halves, *handed, right_root)
    back = local(last_strip_kernel, [smem] + [vmem] * 4, vmem, shape((owners, part, wide), bf16))(
        place, last, right_root, prec, square
    )
    back = lax.all_to_all(back, "fsdp", 0, 0, tiled=True)

    tiles = blocks * (width // 2 // LANES) + 2
    mine = local(select_kernel, [smem, vmem], vmem, shape((tiles, part, LANES), bf16))(block_slot, back)
    near = exchange(mine, NEAR)
    far = exchange(mine, FAR)
    opposite = exchange(near, FAR)
    own = [mine, near, far, opposite]
    other = [twin(x) for x in (mine, far, near, opposite)]
    return local(
        functools.partial(finish_kernel, entries=height * width),
        [smem] + [vmem] * 8,
        pl.BlockSpec(memory_space=pl.ANY),
        shape((mats, rows, full), bf16),
        [
            pltpu.VMEM((mats, rows, full), bf16),
            pltpu.VMEM((blocks, part, LANES), f32),
            pltpu.SemaphoreType.DMA((mats,)),
        ],
    )(place, *own, *other)


def solution(mesh):
    in_specs = (P("replica", None, "fsdp", None), P("fsdp", None, None), P("fsdp", None, None), P())
    return jax.shard_map(
        on_device, mesh=mesh, in_specs=in_specs, out_specs=P(None, "fsdp", None), check_vma=False
    )
```
